32 devices in a mesh: segment: 4 (over x, core), seq: 8 (over z, y).
Axes of the slice: x: 2, y: 2, z: 4, core: 2. Of those that a mesh axis runs over, the one named last changes fastest.
Arguments:
- latent: bfloat16 [3072, 1536], P('seq'), may hold values from -4 to 4
- stale_kv: bfloat16 [4, 2, 3072, 1536], P('segment', None, 'seq'), may hold values from -3 to 3
- query_weight: bfloat16 [4, 1536, 1536], P('segment', 'seq'), may hold values from -0.15625 to 0.15625
- key_weight: bfloat16 [4, 1536, 1536], P('segment', 'seq'), may hold values from -0.15625 to 0.15625
- value_weight: bfloat16 [4, 1536, 1536], P('segment', 'seq'), may hold values from -0.15625 to 0.15625
- out_weight: bfloat16 [4, 1536, 1536], P('segment', 'seq'), may hold values from -0.3125 to 0.3125
- query_gain: float32 [4, 128], P('segment'), may hold values from 0.5 to 2
- key_gain: float32 [4, 128], P('segment'), may hold values from 0.5 to 2
- tile_mask: int32 [48, 6], P('seq'), may hold values from -1 to 47, as said below
Outputs:
- section_out: bfloat16 [4, 3072, 1536], P('segment', 'seq')
The draws below stay inside these ranges and needn't reach their ends.
Inputs may be any that keep to these rules, and one draw needn't show every extreme that they name: `tile_mask`: row g lists the key tiles of query tile g: slot 0 holds g itself, the next slots distinct other tiles whose tile-frame (tile number // 6) differs from that of g by at most one, and the remaining slots -1. Every row lists two or more tiles, and some row lists 6.
All inputs are finite; a program needn't handle non-finite values.
Results may differ from the reference program's by a relative error of at most 0.027.
Values may be sent and summed in bfloat16 or wider, within the bound.
A program may use at most 128 MiB of HBM per device.

```python
import math
import jax
import jax.numpy as jnp
from jax import lax

D = 1536
HEADS = 12
HEAD = 128
TILE = 64
KT = 6
PATCHES = 3
TPP = 2
TPD = 6
NTILES = 48
TOKENS = 3072
N_SEGMENT = 4
N_SEQ = 8


def draw_tile_mask(key, part):
    key_score, key_count = jax.random.split(key)
    query = jnp.arange(NTILES, dtype=jnp.int32)
    frame_of = query // TPD
    candidate = jnp.arange(3 * TPD, dtype=jnp.int32)
    tile_ids = (frame_of[:, None] - 1) * TPD + candidate[None, :]
    allowed = (tile_ids >= 0) & (tile_ids < NTILES) & (tile_ids != query[:, None])
    scores = jax.random.randint(key_score, (NTILES, 3 * TPD), 0, 1 << 20, dtype=jnp.int32) * 256 + candidate[None, :]
    scores = jnp.where(allowed, scores, -1)
    unused, picks = lax.top_k(scores, KT - 1)
    chosen = jnp.take_along_axis(tile_ids, picks, axis=1)
    counts = jax.random.randint(key_count, (NTILES,), 2, KT + 1, dtype=jnp.int32)
    counts = counts.at[0].set(KT).at[1].set(2)
    listed = jnp.concatenate([query[:, None], chosen], axis=1)
    slots = jnp.arange(KT, dtype=jnp.int32)
    return jnp.where(slots[None, :] < counts[:, None], listed, -1).astype(jnp.int32)


def level_of(key, shape, cuts, smallest, largest):
    level = 1.0
    for dim, blocks in cuts:
        draws = jax.random.uniform(jax.random.fold_in(jax.random.fold_in(key, 6), dim), (blocks,), jnp.float32, smallest / len(cuts), largest / len(cuts))
        level = level * jnp.repeat(jnp.exp(draws), shape[dim] // blocks).reshape((-1,) + (1,) * (len(shape) - 1 - dim))
    return level


def bell_draw(own_key, shape, scale, most, shards=(), kind=jnp.bfloat16):
    drawn = scale * jax.random.normal(own_key, shape, jnp.float32)
    if shards:
        drawn = drawn * level_of(own_key, shape, shards, -0.22, 0.18)
    return jnp.clip(drawn, -most, most).astype(kind)


def setup_inputs(seed: int = 0) -> dict:
    key_of = jax.random.split(jax.random.key(seed), 10)
    return {
        "latent": bell_draw(key_of[0], (TOKENS, D), 1.0, 4.0, ((0, 8),)),
        "stale_kv": bell_draw(key_of[1], (N_SEGMENT, 2, TOKENS, D), 1.0, 3.0, ((0, 4), (2, 8))),
        "query_weight": bell_draw(key_of[2], (N_SEGMENT, D, D), D ** -0.5, 0.15625, ((0, 4), (1, 8))),
        "key_weight": bell_draw(key_of[3], (N_SEGMENT, D, D), D ** -0.5, 0.15625, ((0, 4), (1, 8))),
        "value_weight": bell_draw(key_of[4], (N_SEGMENT, D, D), D ** -0.5, 0.15625, ((0, 4), (1, 8))),
        "out_weight": bell_draw(key_of[5], (N_SEGMENT, D, D), (2.0 / D ** 0.5), 0.3125, ((0, 4), (1, 8))),
        "query_gain": jnp.clip(jnp.exp(math.log(2.0) - 1.3862944 * jax.random.uniform(key_of[6], (N_SEGMENT, HEAD), jnp.float32) ** level_of(key_of[6], (N_SEGMENT, HEAD), ((0, 4),), -0.2, 0.2)), 0.5, 2.0),
        "key_gain": jnp.clip(jnp.exp(math.log(2.0) - 1.3862944 * jax.random.uniform(key_of[7], (N_SEGMENT, HEAD), jnp.float32) ** level_of(key_of[7], (N_SEGMENT, HEAD), ((0, 4),), -0.2, 0.2)), 0.5, 2.0),
        "tile_mask": draw_tile_mask(jax.random.fold_in(key_of[9], 71), 0),
    }


epsilon = 1e-06

def head_normed(projected, gain):
    n_rows = projected.shape[0]
    heads = projected.reshape(n_rows, HEADS, HEAD)
    scaled = heads * lax.rsqrt(lax.optimization_barrier(jnp.mean(heads * heads, axis=-1, keepdims=True)) + epsilon)
    return (scaled * gain).reshape(n_rows, D).astype(jnp.bfloat16)

def attend(queries, tile_blocks, tile_lists):
    usable = tile_lists >= 0
    tile_index = jnp.where(usable, tile_lists, 0).astype(jnp.int32)
    n_query = tile_lists.shape[0]
    key_heads = tile_blocks[0][tile_index].astype(jnp.float32).reshape(n_query, KT * TILE, HEADS, HEAD)
    value_heads = tile_blocks[1][tile_index].astype(jnp.float32).reshape(n_query, KT * TILE, HEADS, HEAD)
    query_heads = queries.astype(jnp.float32).reshape(n_query, TILE, HEADS, HEAD)
    scores = jnp.einsum('pthe,pkhe->phtk', query_heads, key_heads) / math.sqrt(HEAD)
    listed = jnp.repeat(usable, TILE, axis=1).astype(jnp.float32)
    weights = jnp.exp(scores) * listed[:, None, None, :]
    totals = lax.optimization_barrier(jnp.sum(weights, axis=-1))
    rounded = lax.optimization_barrier(weights.astype(jnp.bfloat16)).astype(jnp.float32)
    summed = jnp.einsum('phtk,pkhe->pthe', rounded, value_heads)
    return summed / jnp.swapaxes(totals, 1, 2)[..., None]

def reference(latent, stale_kv, query_weight, key_weight, value_weight, out_weight, query_gain, key_gain, tile_mask):
    patch_rows = TPP * TILE
    current = latent.reshape(N_SEQ, PATCHES, patch_rows, D)
    lists_all = tile_mask.reshape(N_SEQ, PATCHES, TPP, KT)
    results = []
    for section in range(N_SEGMENT):
        kv_cache = stale_kv[section].reshape(2, N_SEQ, PATCHES, patch_rows, D)
        produced = jnp.zeros_like(current)
        for patch_id in range(PATCHES):
            inputs = current[:, patch_id].reshape(N_SEQ * patch_rows, D)
            fresh_q = head_normed(jnp.dot(inputs, query_weight[section], preferred_element_type=jnp.float32), query_gain[section])
            fresh_k = head_normed(jnp.dot(inputs, key_weight[section], preferred_element_type=jnp.float32), key_gain[section])
            fresh_v = jnp.dot(inputs, value_weight[section], preferred_element_type=jnp.float32).astype(jnp.bfloat16)
            kv_cache = kv_cache.at[0, :, patch_id].set(fresh_k.reshape(N_SEQ, patch_rows, D))
            kv_cache = kv_cache.at[1, :, patch_id].set(fresh_v.reshape(N_SEQ, patch_rows, D))
            tile_blocks = kv_cache.reshape(2, NTILES, TILE, D)
            tile_lists = lists_all[:, patch_id].reshape(N_SEQ * TPP, KT)
            attention = attend(fresh_q.reshape(N_SEQ * TPP, TILE, D), tile_blocks, tile_lists)
            attention_b = attention.reshape(N_SEQ * patch_rows, D).astype(jnp.bfloat16)
            mixed = jnp.dot(attention_b, out_weight[section], preferred_element_type=jnp.float32)
            leaving = (inputs.astype(jnp.float32) + mixed).astype(jnp.bfloat16)
            produced = produced.at[:, patch_id].set(leaving.reshape(N_SEQ, patch_rows, D))
        results.append(produced.reshape(TOKENS, D))
        current = produced
    return jnp.stack(results)
```

```python
import functools
import math

import jax
import jax.numpy as jnp
from jax import lax
from jax.experimental import pallas as pl
from jax.experimental.pallas import tpu as pltpu
from jax.sharding import PartitionSpec as P

D = 1536
HEADS = 12
HEAD = 128
TILE = 64
PATCHES = 3
TPP = 2
TPD = PATCHES * TPP
WIDE = 256
CHUNKS = D // WIDE
LANE_CHUNKS = CHUNKS // 2
MATS = 4
EPSILON = 1e-06
MESH = pl.DeviceIdType.MESH


def head_normed(projected, gain):
    mean = jnp.mean(projected * projected, axis=-1, keepdims=True)
    return (projected * lax.rsqrt(mean + EPSILON) * gain).astype(jnp.bfloat16)


def ring_place(seq, n):
    half = seq // 2
    return jnp.where(seq % 2 == 0, half, n - 1 - half)


def ring_seq(place, n):
    return jnp.where(place < n // 2, 2 * place, 2 * (n - 1 - place) + 1)


def kernel(
    n_seg,
    n_seq,
    tidx_ref,
    listed_ref,
    gain_q_ref,
    gain_k_ref,
    latent_ref,
    stale_ref,
    wq_ref,
    wk_ref,
    wv_ref,
    wo_ref,
    out_ref,
    weights,
    kv,
    xbuf,
    attn,
    load_sem,
    own_sem,
    ring_send,
    ring_recv,
    stale_send,
    stale_recv,
    x_send,
    x_recv,
):
    seg = lax.axis_index("segment")
    seq = lax.axis_index("seq")
    depth = wq_ref.shape[0]
    patch_rows = xbuf.shape[2]
    has_left = seq > 0
    has_right = seq < n_seq - 1
    has_next = seg < n_seg - 1
    has_prev = seg > 0
    place = ring_place(seq, n_seq)
    ring_right = ring_seq(lax.rem(place + 1, n_seq), n_seq)
    ring_left = ring_seq(lax.rem(place + n_seq - 1, n_seq), n_seq)

    mine = pl.ds(pl.multiple_of(seq * depth, 16), depth)
    loads = []
    for mat, ref in enumerate((wq_ref, wk_ref, wv_ref, wo_ref)):
        for c in range(CHUNKS):
            loads.append(
                pltpu.make_async_copy(
                    ref.at[:, pl.ds(c * WIDE, WIDE)],
                    weights.at[c, mat, mine, :],
                    load_sem.at[mat * CHUNKS + c],
                )
            )
    for load in loads:
        load.start()
    own_stale = pltpu.make_async_copy(
        stale_ref.at[:, pl.ds(TPP, TPD - TPP)],
        kv.at[:, pl.ds(TPD + TPP, TPD - TPP)],
        own_sem,
    )
    own_stale.start()

    @pl.when(jnp.logical_not(has_left))
    def _():
        xbuf[:, 0] = jnp.zeros((PATCHES, patch_rows, D), jnp.bfloat16)

    @pl.when(jnp.logical_not(has_right))
    def _():
        xbuf[:, 2] = jnp.zeros((PATCHES, patch_rows, D), jnp.bfloat16)

    @pl.when(seg == 0)
    def _():
        xbuf[:, 1] = latent_ref[...]

    barrier = pltpu.get_barrier_semaphore()
    sides = ((-1, has_left), (0, None), (1, has_right))

    def greet(to_seg, to_seq):
        pl.semaphore_signal(barrier, inc=1, device_id=(to_seg, to_seq), device_id_type=MESH)

    greet(seg, ring_right)
    greet(seg, ring_left)
    pl.when(has_left)(lambda: greet(seg, seq - 1))
    pl.when(has_right)(lambda: greet(seg, seq + 1))
    for by, there in sides:
        ahead = has_next if there is None else jnp.logical_and(has_next, there)
        behind = has_prev if there is None else jnp.logical_and(has_prev, there)
        pl.when(ahead)(functools.partial(greet, seg + 1, seq + by))
        pl.when(behind)(functools.partial(greet, seg - 1, seq + by))
    beside = has_left.astype(jnp.int32) + has_right.astype(jnp.int32)
    levels = has_next.astype(jnp.int32) + has_prev.astype(jnp.int32)
    pl.semaphore_wait(barrier, 2 + beside + levels * (1 + beside))

    def x_copy(src, patch, by, to_seg):
        return pltpu.make_async_remote_copy(
            src_ref=src.at[patch],
            dst_ref=xbuf.at[patch, 1 - by],
            send_sem=x_send.at[patch, 1 - by],
            recv_sem=x_recv.at[patch, 1 - by],
            device_id=(to_seg, seq + by),
            device_id_type=MESH,
        )

    def stale_copy(by):
        return pltpu.make_async_remote_copy(
            src_ref=stale_ref.at[:, pl.ds(TPP, TPD - TPP)],
            dst_ref=kv.at[:, pl.ds((1 - by) * TPD + TPP, TPD - TPP)],
            send_sem=stale_send.at[1 - by],
            recv_sem=stale_recv.at[1 - by],
            device_id=(seg, seq + by),
            device_id_type=MESH,
        )

    def ring_copy(step, way, part):
        owner = lax.rem(place + (n_seq - step if way == 0 else step), n_seq)
        rows = pl.ds(pl.multiple_of(ring_seq(owner, n_seq) * depth, 16), depth)
        block = weights.at[way * LANE_CHUNKS + part, :, rows, :]
        return pltpu.make_async_remote_copy(
            src_ref=block,
            dst_ref=block,
            send_sem=ring_send.at[way, step, part],
            recv_sem=ring_recv.at[way, step, part],
            device_id=(seg, ring_right if way == 0 else ring_left),
            device_id_type=MESH,
        )

    def ring_arrival(step, way, part):
        owner = lax.rem(place + (n_seq - step - 1 if way == 0 else step + 1), n_seq)
        rows = pl.ds(pl.multiple_of(ring_seq(owner, n_seq) * depth, 16), depth)
        block = weights.at[way * LANE_CHUNKS + part, :, rows, :]
        return pltpu.make_async_remote_copy(
            src_ref=block,
            dst_ref=block,
            send_sem=ring_send.at[way, step, part],
            recv_sem=ring_recv.at[way, step, part],
            device_id=(seg, ring_right if way == 0 else ring_left),
            device_id_type=MESH,
        )

    parts = [(part, way) for part in range(LANE_CHUNKS) for way in range(2)]
    for load in loads:
        load.wait()
    for part, way in parts:
        ring_copy(0, way, part).start()

    def send_latent(patch, carry):
        pl.when(has_left)(lambda: x_copy(latent_ref, patch, -1, seg).start())
        pl.when(has_right)(lambda: x_copy(latent_ref, patch, 1, seg).start())
        return carry

    @pl.when(seg == 0)
    def _():
        lax.fori_loop(0, PATCHES, send_latent, 0)

    pl.when(has_left)(lambda: stale_copy(-1).start())
    pl.when(has_right)(lambda: stale_copy(1).start())

    def forward(step, carry):
        for part, way in parts:
            ring_arrival(step - 1, way, part).wait_recv()
            ring_copy(step, way, part).start()
        return carry

    lax.fori_loop(1, n_seq - 1, forward, 0)
    for part, way in parts:
        ring_arrival(n_seq - 2, way, part).wait_recv()

    own_stale.wait()
    pl.when(has_left)(lambda: stale_copy(1).wait_recv())
    pl.when(has_right)(lambda: stale_copy(-1).wait_recv())

    gain_q = gain_q_ref[...]
    gain_k = gain_k_ref[...]

    def do_patch(patch, carry):
        pl.when(has_left)(lambda: x_copy(out_ref, patch, 1, seg).wait_recv())
        pl.when(has_right)(lambda: x_copy(out_ref, patch, -1, seg).wait_recv())
        pl.when(has_prev)(lambda: x_copy(out_ref, patch, 0, seg).wait_recv())

        def do_heads(c, inner):
            columns = pl.ds(pl.multiple_of(c * WIDE, WIDE), WIDE)
            rows3 = xbuf[patch].reshape(3 * patch_rows, D)
            q = jnp.dot(xbuf[patch, 1], weights[c, 0], preferred_element_type=jnp.float32)
            k = jnp.dot(rows3, weights[c, 1], preferred_element_type=jnp.float32)
            v = jnp.dot(rows3, weights[c, 2], preferred_element_type=jnp.float32)
            fresh_q, fresh_k = [], []
            for h in range(WIDE // HEAD):
                lanes = slice(h * HEAD, (h + 1) * HEAD)
                fresh_q.append(head_normed(q[:, lanes], gain_q))
                fresh_k.append(head_normed(k[:, lanes], gain_k))
            fresh_k = jnp.concatenate(fresh_k, axis=1).reshape(3, TPP, TILE, WIDE)
            fresh_v = v.astype(jnp.bfloat16).reshape(3, TPP, TILE, WIDE)
            for f in range(3):
                tiles = pl.ds(f * TPD + patch * TPP, TPP)
                kv[0, tiles, :, columns] = fresh_k[f]
                kv[1, tiles, :, columns] = fresh_v[f]
            for i in range(TPP):
                g = patch * TPP + i
                places = [tidx_ref[g, m] for m in range(TPD)]
                listed = listed_ref[g]
                keys = jnp.concatenate([kv[0, t, :, columns] for t in places], axis=0)
                values = jnp.concatenate([kv[1, t, :, columns] for t in places], axis=0)
                for h in range(WIDE // HEAD):
                    lanes = slice(h * HEAD, (h + 1) * HEAD)
                    score = lax.dot_general(
                        fresh_q[h][i * TILE : (i + 1) * TILE],
                        keys[:, lanes],
                        (((1,), (1,)), ((), ())),
                        preferred_element_type=jnp.float32,
                    )
                    weight = jnp.exp(score * (1.0 / math.sqrt(HEAD))) * listed
                    total = jnp.sum(weight, axis=-1, keepdims=True)
                    summed = jnp.dot(
                        weight.astype(jnp.bfloat16),
                        values[:, lanes],
                        preferred_element_type=jnp.float32,
                    )
                    spot = pl.ds(pl.multiple_of(c * WIDE + h * HEAD, HEAD), HEAD)
                    attn[i * TILE : (i + 1) * TILE, spot] = (summed / total).astype(jnp.bfloat16)
            return inner

        lax.fori_loop(0, CHUNKS, do_heads, 0)

        def do_out(c, inner):
            columns = pl.ds(pl.multiple_of(c * WIDE, WIDE), WIDE)
            mixed = jnp.dot(attn[...], weights[c, 3], preferred_element_type=jnp.float32)
            entering = xbuf[patch, 1, :, columns].astype(jnp.float32)
            out_ref[patch, :, columns] = (entering + mixed).astype(jnp.bfloat16)
            return inner

        lax.fori_loop(0, CHUNKS, do_out, 0)

        @pl.when(has_next)
        def _():
            x_copy(out_ref, patch, 0, seg + 1).start()
            pl.when(has_left)(lambda: x_copy(out_ref, patch, -1, seg + 1).start())
            pl.when(has_right)(lambda: x_copy(out_ref, patch, 1, seg + 1).start())

        return carry

    def latent_left(patch, carry):
        pl.when(has_left)(lambda: x_copy(latent_ref, patch, -1, seg).wait_send())
        pl.when(has_right)(lambda: x_copy(latent_ref, patch, 1, seg).wait_send())
        return carry

    @pl.when(seg == 0)
    def _():
        lax.fori_loop(0, PATCHES, latent_left, 0)

    lax.fori_loop(0, PATCHES, do_patch, 0)

    def drain_ring(step, carry):
        for part, way in parts:
            ring_copy(step, way, part).wait_send()
        return carry

    lax.fori_loop(0, n_seq - 1, drain_ring, 0)
    pl.when(has_left)(lambda: stale_copy(-1).wait_send())
    pl.when(has_right)(lambda: stale_copy(1).wait_send())

    def drain_x(patch, carry):
        x_copy(out_ref, patch, 0, seg + 1).wait_send()
        pl.when(has_left)(lambda: x_copy(out_ref, patch, -1, seg + 1).wait_send())
        pl.when(has_right)(lambda: x_copy(out_ref, patch, 1, seg + 1).wait_send())
        return carry

    @pl.when(has_next)
    def _():
        lax.fori_loop(0, PATCHES, drain_x, 0)


def per_device(
    n_seg,
    n_seq,
    latent,
    stale_kv,
    query_weight,
    key_weight,
    value_weight,
    out_weight,
    query_gain,
    key_gain,
    tile_mask,
):
    tok_dev = latent.shape[0]
    patch_rows = tok_dev // PATCHES
    tiles_dev = tile_mask.shape[0]
    seq = lax.axis_index("seq")
    usable = tile_mask >= 0
    own = tiles_dev + jnp.arange(tiles_dev, dtype=jnp.int32)[:, None]
    tidx = jnp.where(usable, tile_mask - (seq - 1) * tiles_dev, own)
    listed = jnp.repeat(usable, TILE, axis=1).astype(jnp.float32)[:, None, :]
    vmem = pl.BlockSpec(memory_space=pltpu.VMEM)
    smem = pl.BlockSpec(memory_space=pltpu.SMEM)
    anywhere = pl.BlockSpec(memory_space=pl.ANY)
    steps = n_seq - 1
    dma = pltpu.SemaphoreType.DMA
    result = pl.pallas_call(
        functools.partial(kernel, n_seg, n_seq),
        out_shape=jax.ShapeDtypeStruct((PATCHES, patch_rows, D), jnp.bfloat16),
        in_specs=[smem, vmem, vmem, vmem, vmem] + [anywhere] * 5,
        out_specs=vmem,
        scratch_shapes=[
            pltpu.VMEM((CHUNKS, MATS, D, WIDE), jnp.bfloat16),
            pltpu.VMEM((2, 3 * tiles_dev, TILE, D), jnp.bfloat16),
            pltpu.VMEM((PATCHES, 3, patch_rows, D), jnp.bfloat16),
            pltpu.VMEM((patch_rows, D), jnp.bfloat16),
            dma((MATS * CHUNKS,)),
            dma,
            dma((2, steps, LANE_CHUNKS)),
            dma((2, steps, LANE_CHUNKS)),
            dma((3,)),
            dma((3,)),
            dma((PATCHES, 3)),
            dma((PATCHES, 3)),
        ],
        compiler_params=pltpu.CompilerParams(
            collective_id=0, has_side_effects=True, vmem_limit_bytes=56 * 1024 * 1024
        ),
    )(
        tidx,
        listed,
        query_gain,
        key_gain,
        latent.reshape(PATCHES, patch_rows, D),
        stale_kv[0].reshape(2, tiles_dev, TILE, D),
        query_weight[0],
        key_weight[0],
        value_weight[0],
        out_weight[0],
    )
    return result.reshape(1, tok_dev, D)


def solution(mesh):
    return jax.shard_map(
        functools.partial(per_device, mesh.shape["segment"], mesh.shape["seq"]),
        mesh=mesh,
        in_specs=(
            P("seq", None),
            P("segment", None, "seq", None),
            P("segment", "seq", None),
            P("segment", "seq", None),
            P("segment", "seq", None),
            P("segment", "seq", None),
            P("segment", None),
            P("segment", None),
            P("seq", None),
        ),
        out_specs=P("segment", "seq", None),
        check_vma=False,
    )
```

```python
import functools
import math

import jax
import jax.numpy as jnp
from jax import lax
from jax.experimental import pallas as pl
from jax.experimental.pallas import tpu as pltpu
from jax.sharding import PartitionSpec as P

D = 1536
HEADS = 12
HEAD = 128
TILE = 64
PATCHES = 3
TPP = 2
TPD = PATCHES * TPP
WIDE = 256
CHUNKS = D // WIDE
LANE_CHUNKS = CHUNKS // 2
MATS = 4
EPSILON = 1e-06
MESH = pl.DeviceIdType.MESH


def head_normed(projected, gain):
    mean = jnp.mean(projected * projected, axis=-1, keepdims=True)
    return (projected * lax.rsqrt(mean + EPSILON) * gain).astype(jnp.bfloat16)


def ring_place(seq, n):
    half = seq // 2
    return jnp.where(seq % 2 == 0, half, n - 1 - half)


def ring_seq(place, n):
    return jnp.where(place < n // 2, 2 * place, 2 * (n - 1 - place) + 1)


def kernel(
    n_seg,
    n_seq,
    tidx_ref,
    listed_ref,
    gain_q_ref,
    gain_k_ref,
    latent_ref,
    stale_ref,
    wq_ref,
    wk_ref,
    wv_ref,
    wo_ref,
    out_ref,
    weights,
    kv,
    xbuf,
    attn,
    load_sem,
    own_sem,
    ring_send,
    ring_recv,
    last_send,
    last_recv,
    go_sem,
    stale_send,
    stale_recv,
    x_send,
    x_recv,
):
    seg = lax.axis_index("segment")
    seq = lax.axis_index("seq")
    depth = wq_ref.shape[0]
    patch_rows = xbuf.shape[2]
    has_left = seq > 0
    has_right = seq < n_seq - 1
    has_next = seg < n_seg - 1
    has_prev = seg > 0
    place = ring_place(seq, n_seq)
    ring_right = ring_seq(lax.rem(place + 1, n_seq), n_seq)
    ring_left = ring_seq(lax.rem(place + n_seq - 1, n_seq), n_seq)

    mine = pl.ds(pl.multiple_of(seq * depth, 16), depth)
    loads = []
    for mat, ref in enumerate((wq_ref, wk_ref, wv_ref, wo_ref)):
        for c in range(CHUNKS):
            loads.append(
                pltpu.make_async_copy(
                    ref.at[:, pl.ds(c * WIDE, WIDE)],
                    weights.at[c, mat, mine, :],
                    load_sem.at[mat * CHUNKS + c],
                )
            )
    for load in loads:
        load.start()
    own_stale = pltpu.make_async_copy(
        stale_ref.at[:, pl.ds(TPP, TPD - TPP)],
        kv.at[:, pl.ds(TPD + TPP, TPD - TPP)],
        own_sem,
    )
    own_stale.start()

    @pl.when(jnp.logical_not(has_left))
    def _():
        xbuf[:, 0] = jnp.zeros((PATCHES, patch_rows, D), jnp.bfloat16)

    @pl.when(jnp.logical_not(has_right))
    def _():
        xbuf[:, 2] = jnp.zeros((PATCHES, patch_rows, D), jnp.bfloat16)

    @pl.when(seg == 0)
    def _():
        xbuf[:, 1] = latent_ref[...]

    barrier = pltpu.get_barrier_semaphore()
    sides = ((-1, has_left), (0, None), (1, has_right))

    def greet(to_seg, to_seq):
        pl.semaphore_signal(barrier, inc=1, device_id=(to_seg, to_seq), device_id_type=MESH)

    greet(seg, ring_right)
    greet(seg, ring_left)
    pl.when(has_left)(lambda: greet(seg, seq - 1))
    pl.when(has_right)(lambda: greet(seg, seq + 1))
    for by, there in sides:
        ahead = has_next if there is None else jnp.logical_and(has_next, there)
        behind = has_prev if there is None else jnp.logical_and(has_prev, there)
        pl.when(ahead)(functools.partial(greet, seg + 1, seq + by))
        pl.when(behind)(functools.partial(greet, seg - 1, seq + by))
    beside = has_left.astype(jnp.int32) + has_right.astype(jnp.int32)
    levels = has_next.astype(jnp.int32) + has_prev.astype(jnp.int32)
    pl.semaphore_wait(barrier, 2 + beside + levels * (1 + beside))

    def x_copy(src, patch, by, to_seg):
        return pltpu.make_async_remote_copy(
            src_ref=src.at[patch],
            dst_ref=xbuf.at[patch, 1 - by],
            send_sem=x_send.at[patch, 1 - by],
            recv_sem=x_recv.at[patch, 1 - by],
            device_id=(to_seg, seq + by),
            device_id_type=MESH,
        )

    def stale_copy(by):
        return pltpu.make_async_remote_copy(
            src_ref=stale_ref.at[:, pl.ds(TPP, TPD - TPP)],
            dst_ref=kv.at[:, pl.ds((1 - by) * TPD + TPP, TPD - TPP)],
            send_sem=stale_send.at[1 - by],
            recv_sem=stale_recv.at[1 - by],
            device_id=(seg, seq + by),
            device_id_type=MESH,
        )

    def ring_send_to(way, block, send_sem, recv_sem):
        return pltpu.make_async_remote_copy(
            src_ref=block,
            dst_ref=block,
            send_sem=send_sem,
            recv_sem=recv_sem,
            device_id=(seg, ring_right if way == 0 else ring_left),
            device_id_type=MESH,
        )

    def ring_rows(step, way, late):
        owner = lax.rem(place + (n_seq - step - late if way == 0 else step + late), n_seq)
        return pl.ds(pl.multiple_of(ring_seq(owner, n_seq) * depth, 16), depth)

    def ring_copy(step, way, part, late=0):
        rows = ring_rows(step, way, late)
        block = weights.at[way * LANE_CHUNKS + part, pl.ds(0, MATS - 1), rows, :]
        return ring_send_to(way, block, ring_send.at[way, step, part], ring_recv.at[way, step, part])

    def last_copy(step, way, late=0):
        rows = ring_rows(step, way, late)
        block = weights.at[pl.ds(way * LANE_CHUNKS, LANE_CHUNKS), MATS - 1, rows, :]
        return ring_send_to(way, block, last_send.at[way, step], last_recv.at[way, step])

    parts = [(part, way) for part in range(LANE_CHUNKS) for way in range(2)]
    odd = lax.rem(seg, 2) == 1
    for load in loads:
        load.wait()

    def send_latent(patch, carry):
        pl.when(has_left)(lambda: x_copy(latent_ref, patch, -1, seg).start())
        pl.when(has_right)(lambda: x_copy(latent_ref, patch, 1, seg).start())
        return carry

    @pl.when(seg == 0)
    def _():
        lax.fori_loop(0, PATCHES, send_latent, 0)

    pl.when(has_left)(lambda: stale_copy(-1).start())
    pl.when(has_right)(lambda: stale_copy(1).start())

    pl.when(odd)(lambda: pl.semaphore_wait(go_sem, 1))
    for part, way in parts:
        ring_copy(0, way, part).start()

    def forward(step, carry):
        for part, way in parts:
            ring_copy(step - 1, way, part, 1).wait_recv()
            ring_copy(step, way, part).start()
        return carry

    lax.fori_loop(1, n_seq - 1, forward, 0)
    for way in range(2):
        last_copy(0, way).start()
    for part, way in parts:
        ring_copy(n_seq - 2, way, part, 1).wait_recv()

    @pl.when(jnp.logical_not(odd))
    def _():
        pl.semaphore_signal(go_sem, inc=1, device_id=(seg + 1, seq), device_id_type=MESH)

    def forward_last(step, carry):
        for way in range(2):
            last_copy(step - 1, way, 1).wait_recv()
            last_copy(step, way).start()
        return carry

    def finish_last():
        for way in range(2):
            last_copy(n_seq - 2, way, 1).wait_recv()

    early = seg < 2
    per_chunk = pl.cdiv(n_seq - 2, CHUNKS)

    @pl.when(jnp.logical_not(early))
    def _():
        lax.fori_loop(1, n_seq - 1, forward_last, 0)
        finish_last()

    own_stale.wait()
    pl.when(has_left)(lambda: stale_copy(1).wait_recv())
    pl.when(has_right)(lambda: stale_copy(-1).wait_recv())

    gain_q = gain_q_ref[...]
    gain_k = gain_k_ref[...]

    def do_patch(patch, carry):
        pl.when(has_left)(lambda: x_copy(out_ref, patch, 1, seg).wait_recv())
        pl.when(has_right)(lambda: x_copy(out_ref, patch, -1, seg).wait_recv())
        pl.when(has_prev)(lambda: x_copy(out_ref, patch, 0, seg).wait_recv())

        beside_last = jnp.logical_and(early, patch == 0)

        def do_heads(c, inner):
            @pl.when(beside_last)
            def _():
                first = 1 + c * per_chunk
                until = jnp.minimum(first + per_chunk, n_seq - 1)
                lax.fori_loop(first, until, forward_last, 0)

            columns = pl.ds(pl.multiple_of(c * WIDE, WIDE), WIDE)
            rows3 = xbuf[patch].reshape(3 * patch_rows, D)
            q = jnp.dot(xbuf[patch, 1], weights[c, 0], preferred_element_type=jnp.float32)
            k = jnp.dot(rows3, weights[c, 1], preferred_element_type=jnp.float32)
            v = jnp.dot(rows3, weights[c, 2], preferred_element_type=jnp.float32)
            fresh_q, fresh_k = [], []
            for h in range(WIDE // HEAD):
                lanes = slice(h * HEAD, (h + 1) * HEAD)
                fresh_q.append(head_normed(q[:, lanes], gain_q))
                fresh_k.append(head_normed(k[:, lanes], gain_k))
            fresh_k = jnp.concatenate(fresh_k, axis=1).reshape(3, TPP, TILE, WIDE)
            fresh_v = v.astype(jnp.bfloat16).reshape(3, TPP, TILE, WIDE)
            for f in range(3):
                tiles = pl.ds(f * TPD + patch * TPP, TPP)
                kv[0, tiles, :, columns] = fresh_k[f]
                kv[1, tiles, :, columns] = fresh_v[f]
            for i in range(TPP):
                g = patch * TPP + i
                places = [tidx_ref[g, m] for m in range(TPD)]
                listed = listed_ref[g]
                keys = jnp.concatenate([kv[0, t, :, columns] for t in places], axis=0)
                values = jnp.concatenate([kv[1, t, :, columns] for t in places], axis=0)
                for h in range(WIDE // HEAD):
                    lanes = slice(h * HEAD, (h + 1) * HEAD)
                    score = lax.dot_general(
                        fresh_q[h][i * TILE : (i + 1) * TILE],
                        keys[:, lanes],
                        (((1,), (1,)), ((), ())),
                        preferred_element_type=jnp.float32,
                    )
                    weight = jnp.exp(score * (1.0 / math.sqrt(HEAD))) * listed
                    total = jnp.sum(weight, axis=-1, keepdims=True)
                    summed = jnp.dot(
                        weight.astype(jnp.bfloat16),
                        values[:, lanes],
                        preferred_element_type=jnp.float32,
                    )
                    spot = pl.ds(pl.multiple_of(c * WIDE + h * HEAD, HEAD), HEAD)
                    attn[i * TILE : (i + 1) * TILE, spot] = (summed / total).astype(jnp.bfloat16)
            return inner

        lax.fori_loop(0, CHUNKS, do_heads, 0)

        pl.when(beside_last)(finish_last)

        def do_out(c, inner):
            columns = pl.ds(pl.multiple_of(c * WIDE, WIDE), WIDE)
            mixed = jnp.dot(attn[...], weights[c, 3], preferred_element_type=jnp.float32)
            entering = xbuf[patch, 1, :, columns].astype(jnp.float32)
            out_ref[patch, :, columns] = (entering + mixed).astype(jnp.bfloat16)
            return inner

        lax.fori_loop(0, CHUNKS, do_out, 0)

        @pl.when(has_next)
        def _():
            pl.when(has_left)(lambda: x_copy(out_ref, patch, -1, seg + 1).start())
            pl.when(has_right)(lambda: x_copy(out_ref, patch, 1, seg + 1).start())
            x_copy(out_ref, patch, 0, seg + 1).start()

        return carry

    def latent_left(patch, carry):
        pl.when(has_left)(lambda: x_copy(latent_ref, patch, -1, seg).wait_send())
        pl.when(has_right)(lambda: x_copy(latent_ref, patch, 1, seg).wait_send())
        return carry

    @pl.when(seg == 0)
    def _():
        lax.fori_loop(0, PATCHES, latent_left, 0)

    lax.fori_loop(0, PATCHES, do_patch, 0)

    def drain_ring(step, carry):
        for part, way in parts:
            ring_copy(step, way, part).wait_send()
        for way in range(2):
            last_copy(step, way).wait_send()
        return carry

    lax.fori_loop(0, n_seq - 1, drain_ring, 0)
    pl.when(has_left)(lambda: stale_copy(-1).wait_send())
    pl.when(has_right)(lambda: stale_copy(1).wait_send())

    def drain_x(patch, carry):
        x_copy(out_ref, patch, 0, seg + 1).wait_send()
        pl.when(has_left)(lambda: x_copy(out_ref, patch, -1, seg + 1).wait_send())
        pl.when(has_right)(lambda: x_copy(out_ref, patch, 1, seg + 1).wait_send())
        return carry

    @pl.when(has_next)
    def _():
        lax.fori_loop(0, PATCHES, drain_x, 0)


def per_device(
    n_seg,
    n_seq,
    latent,
    stale_kv,
    query_weight,
    key_weight,
    value_weight,
    out_weight,
    query_gain,
    key_gain,
    tile_mask,
):
    tok_dev = latent.shape[0]
    patch_rows = tok_dev // PATCHES
    tiles_dev = tile_mask.shape[0]
    seq = lax.axis_index("seq")
    usable = tile_mask >= 0
    own = tiles_dev + jnp.arange(tiles_dev, dtype=jnp.int32)[:, None]
    tidx = jnp.where(usable, tile_mask - (seq - 1) * tiles_dev, own)
    listed = jnp.repeat(usable, TILE, axis=1).astype(jnp.float32)[:, None, :]
    vmem = pl.BlockSpec(memory_space=pltpu.VMEM)
    smem = pl.BlockSpec(memory_space=pltpu.SMEM)
    anywhere = pl.BlockSpec(memory_space=pl.ANY)
    steps = n_seq - 1
    dma = pltpu.SemaphoreType.DMA
    result = pl.pallas_call(
        functools.partial(kernel, n_seg, n_seq),
        out_shape=jax.ShapeDtypeStruct((PATCHES, patch_rows, D), jnp.bfloat16),
        in_specs=[smem, vmem, vmem, vmem, vmem] + [anywhere] * 5,
        out_specs=vmem,
        scratch_shapes=[
            pltpu.VMEM((CHUNKS, MATS, D, WIDE), jnp.bfloat16),
            pltpu.VMEM((2, 3 * tiles_dev, TILE, D), jnp.bfloat16),
            pltpu.VMEM((PATCHES, 3, patch_rows, D), jnp.bfloat16),
            pltpu.VMEM((patch_rows, D), jnp.bfloat16),
            dma((MATS * CHUNKS,)),
            dma,
            dma((2, steps, LANE_CHUNKS)),
            dma((2, steps, LANE_CHUNKS)),
            dma((2, steps)),
            dma((2, steps)),
            pltpu.SemaphoreType.REGULAR,
            dma((3,)),
            dma((3,)),
            dma((PATCHES, 3)),
            dma((PATCHES, 3)),
        ],
        compiler_params=pltpu.CompilerParams(
            collective_id=0, has_side_effects=True, vmem_limit_bytes=56 * 1024 * 1024
        ),
    )(
        tidx,
        listed,
        query_gain,
        key_gain,
        latent.reshape(PATCHES, patch_rows, D),
        stale_kv[0].reshape(2, tiles_dev, TILE, D),
        query_weight[0],
        key_weight[0],
        value_weight[0],
        out_weight[0],
    )
    return result.reshape(1, tok_dev, D)


def solution(mesh):
    return jax.shard_map(
        functools.partial(per_device, mesh.shape["segment"], mesh.shape["seq"]),
        mesh=mesh,
        in_specs=(
            P("seq", None),
            P("segment", None, "seq", None),
            P("segment", "seq", None),
            P("segment", "seq", None),
            P("segment", "seq", None),
            P("segment", "seq", None),
            P("segment", None),
            P("segment", None),
            P("seq", None),
        ),
        out_specs=P("segment", "seq", None),
        check_vma=False,
    )
```

```python
import functools
import math

import jax
import jax.numpy as jnp
from jax import lax
from jax.experimental import pallas as pl
from jax.experimental.pallas import tpu as pltpu
from jax.sharding import PartitionSpec as P

D = 1536
HEADS = 12
HEAD = 128
TILE = 64
PATCHES = 3
TPP = 2
TPD = PATCHES * TPP
WIDE = 256
CHUNKS = D // WIDE
LANE_CHUNKS = CHUNKS // 2
MATS = 4
EPSILON = 1e-06
MESH = pl.DeviceIdType.MESH


def head_normed(projected, gain):
    mean = jnp.mean(projected * projected, axis=-1, keepdims=True)
    return (projected * lax.rsqrt(mean + EPSILON) * gain).astype(jnp.bfloat16)


def ring_place(seq, n):
    half = seq // 2
    return jnp.where(seq % 2 == 0, half, n - 1 - half)


def ring_seq(place, n):
    return jnp.where(place < n // 2, 2 * place, 2 * (n - 1 - place) + 1)


def kernel(
    n_seg,
    n_seq,
    tidx_ref,
    listed_ref,
    gain_q_ref,
    gain_k_ref,
    latent_ref,
    stale_ref,
    wq_ref,
    wk_ref,
    wv_ref,
    wo_ref,
    out_ref,
    weights,
    kv,
    xbuf,
    attn,
    queries,
    fresh_q,
    fresh,
    load_sem,
    own_sem,
    ring_send,
    ring_recv,
    last_send,
    last_recv,
    go_sem,
    stale_send,
    stale_recv,
    x_send,
    x_recv,
):
    seg = lax.axis_index("segment")
    seq = lax.axis_index("seq")
    depth = wq_ref.shape[0]
    patch_rows = xbuf.shape[2]
    has_left = seq > 0
    has_right = seq < n_seq - 1
    has_next = seg < n_seg - 1
    has_prev = seg > 0
    place = ring_place(seq, n_seq)
    ring_right = ring_seq(lax.rem(place + 1, n_seq), n_seq)
    ring_left = ring_seq(lax.rem(place + n_seq - 1, n_seq), n_seq)

    mine = pl.ds(pl.multiple_of(seq * depth, 16), depth)
    loads = []
    for mat, ref in enumerate((wq_ref, wk_ref, wv_ref, wo_ref)):
        for c in range(CHUNKS):
            loads.append(
                pltpu.make_async_copy(
                    ref.at[:, pl.ds(c * WIDE, WIDE)],
                    weights.at[c, mat, mine, :],
                    load_sem.at[mat * CHUNKS + c],
                )
            )
    for load in loads:
        load.start()
    own_stale = pltpu.make_async_copy(
        stale_ref.at[:, pl.ds(TPP, TPD - TPP)],
        kv.at[:, pl.ds(TPD + TPP, TPD - TPP)],
        own_sem,
    )
    own_stale.start()

    @pl.when(jnp.logical_not(has_left))
    def _():
        xbuf[:, 0] = jnp.zeros((PATCHES, patch_rows, D), jnp.bfloat16)

    @pl.when(jnp.logical_not(has_right))
    def _():
        xbuf[:, 2] = jnp.zeros((PATCHES, patch_rows, D), jnp.bfloat16)

    @pl.when(seg == 0)
    def _():
        xbuf[:, 1] = latent_ref[...]

    barrier = pltpu.get_barrier_semaphore()
    sides = ((-1, has_left), (0, None), (1, has_right))

    def greet(to_seg, to_seq):
        pl.semaphore_signal(barrier, inc=1, device_id=(to_seg, to_seq), device_id_type=MESH)

    greet(seg, ring_right)
    greet(seg, ring_left)
    pl.when(has_left)(lambda: greet(seg, seq - 1))
    pl.when(has_right)(lambda: greet(seg, seq + 1))
    for by, there in sides:
        ahead = has_next if there is None else jnp.logical_and(has_next, there)
        behind = has_prev if there is None else jnp.logical_and(has_prev, there)
        pl.when(ahead)(functools.partial(greet, seg + 1, seq + by))
        pl.when(behind)(functools.partial(greet, seg - 1, seq + by))
    beside = has_left.astype(jnp.int32) + has_right.astype(jnp.int32)
    levels = has_next.astype(jnp.int32) + has_prev.astype(jnp.int32)
    pl.semaphore_wait(barrier, 2 + beside + levels * (1 + beside))

    def x_copy(src, patch, by, to_seg):
        return pltpu.make_async_remote_copy(
            src_ref=src.at[patch],
            dst_ref=xbuf.at[patch, 1 - by],
            send_sem=x_send.at[patch, 1 - by],
            recv_sem=x_recv.at[patch, 1 - by],
            device_id=(to_seg, seq + by),
            device_id_type=MESH,
        )

    def stale_copy(by):
        return pltpu.make_async_remote_copy(
            src_ref=stale_ref.at[:, pl.ds(TPP, TPD - TPP)],
            dst_ref=kv.at[:, pl.ds((1 - by) * TPD + TPP, TPD - TPP)],
            send_sem=stale_send.at[1 - by],
            recv_sem=stale_recv.at[1 - by],
            device_id=(seg, seq + by),
            device_id_type=MESH,
        )

    def ring_send_to(way, block, send_sem, recv_sem):
        return pltpu.make_async_remote_copy(
            src_ref=block,
            dst_ref=block,
            send_sem=send_sem,
            recv_sem=recv_sem,
            device_id=(seg, ring_right if way == 0 else ring_left),
            device_id_type=MESH,
        )

    def ring_rows(step, way, late):
        owner = lax.rem(place + (n_seq - step - late if way == 0 else step + late), n_seq)
        return pl.ds(pl.multiple_of(ring_seq(owner, n_seq) * depth, 16), depth)

    def ring_copy(step, way, part, late=0):
        rows = ring_rows(step, way, late)
        block = weights.at[way * LANE_CHUNKS + part, pl.ds(0, MATS - 1), rows, :]
        return ring_send_to(way, block, ring_send.at[way, step, part], ring_recv.at[way, step, part])

    def last_copy(step, way, late=0):
        rows = ring_rows(step, way, late)
        block = weights.at[pl.ds(way * LANE_CHUNKS, LANE_CHUNKS), MATS - 1, rows, :]
        return ring_send_to(way, block, last_send.at[way, step], last_recv.at[way, step])

    parts = [(part, way) for part in range(LANE_CHUNKS) for way in range(2)]
    odd = lax.rem(seg, 2) == 1
    for load in loads:
        load.wait()

    def send_latent(patch, carry):
        pl.when(has_left)(lambda: x_copy(latent_ref, patch, -1, seg).start())
        pl.when(has_right)(lambda: x_copy(latent_ref, patch, 1, seg).start())
        return carry

    @pl.when(seg == 0)
    def _():
        lax.fori_loop(0, PATCHES, send_latent, 0)

    pl.when(odd)(lambda: pl.semaphore_wait(go_sem, 1))
    for part, way in parts:
        ring_copy(0, way, part).start()
    pl.when(has_left)(lambda: stale_copy(-1).start())
    pl.when(has_right)(lambda: stale_copy(1).start())

    def forward(step, carry):
        for part, way in parts:
            ring_copy(step - 1, way, part, 1).wait_recv()
            ring_copy(step, way, part).start()

        @pl.when(jnp.logical_and(step == n_seq // 2 - 1, jnp.logical_not(odd)))
        def _():
            pl.semaphore_signal(go_sem, inc=1, device_id=(seg + 1, seq), device_id_type=MESH)

        return carry

    lax.fori_loop(1, n_seq - 1, forward, 0)
    for way in range(2):
        last_copy(0, way).start()
    for part, way in parts:
        ring_copy(n_seq - 2, way, part, 1).wait_recv()

    def forward_last(step, carry):
        for way in range(2):
            last_copy(step - 1, way, 1).wait_recv()
            last_copy(step, way).start()
        return carry

    def finish_last():
        for way in range(2):
            last_copy(n_seq - 2, way, 1).wait_recv()

    early = seg < 2
    per_chunk = pl.cdiv(n_seq - 2, CHUNKS)

    @pl.when(jnp.logical_not(early))
    def _():
        lax.fori_loop(1, n_seq - 1, forward_last, 0)
        finish_last()

    own_stale.wait()
    pl.when(has_left)(lambda: stale_copy(1).wait_recv())
    pl.when(has_right)(lambda: stale_copy(-1).wait_recv())

    gain_q = gain_q_ref[...]
    gain_k = gain_k_ref[...]

    def do_patch(patch, carry):
        pl.when(has_left)(lambda: x_copy(out_ref, patch, 1, seg).wait_recv())
        pl.when(has_right)(lambda: x_copy(out_ref, patch, -1, seg).wait_recv())
        pl.when(has_prev)(lambda: x_copy(out_ref, patch, 0, seg).wait_recv())

        beside_last = jnp.logical_and(early, patch == 0)

        def project(c):
            rows3 = xbuf[patch].reshape(3 * patch_rows, D)
            k = jnp.dot(rows3, weights[c, 1], preferred_element_type=jnp.float32)
            for h in range(WIDE // HEAD):
                lanes = slice(h * HEAD, (h + 1) * HEAD)
                fresh[0, :, lanes] = head_normed(k[:, lanes], gain_k)
            v = jnp.dot(rows3, weights[c, 2], preferred_element_type=jnp.float32)
            fresh[1] = v.astype(jnp.bfloat16)
            q = jnp.dot(xbuf[patch, 1], weights[c, 0], preferred_element_type=jnp.float32)
            for h in range(WIDE // HEAD):
                lanes = slice(h * HEAD, (h + 1) * HEAD)
                fresh_q[:, lanes] = head_normed(q[:, lanes], gain_q)

        def keep(c):
            columns = pl.ds(pl.multiple_of(c * WIDE, WIDE), WIDE)
            queries[...] = fresh_q[...]
            for f in range(3):
                tiles = pl.ds(f * TPD + patch * TPP, TPP)
                rows = slice(f * patch_rows, (f + 1) * patch_rows)
                for which in range(2):
                    kv[which, tiles, :, columns] = fresh[which, rows].reshape(TPP, TILE, WIDE)

        def attend(c):
            columns = pl.ds(pl.multiple_of(c * WIDE, WIDE), WIDE)
            for i in range(TPP):
                g = patch * TPP + i
                places = [tidx_ref[g, m] for m in range(TPD)]
                listed = listed_ref[g]
                keys = jnp.concatenate([kv[0, t, :, columns] for t in places], axis=0)
                values = jnp.concatenate([kv[1, t, :, columns] for t in places], axis=0)
                own = queries[i * TILE : (i + 1) * TILE, :]
                for h in range(WIDE // HEAD):
                    lanes = slice(h * HEAD, (h + 1) * HEAD)
                    score = lax.dot_general(
                        own[:, lanes],
                        keys[:, lanes],
                        (((1,), (1,)), ((), ())),
                        preferred_element_type=jnp.float32,
                    )
                    weight = jnp.exp(score * (1.0 / math.sqrt(HEAD))) * listed
                    total = jnp.sum(weight, axis=-1, keepdims=True)
                    summed = jnp.dot(
                        weight.astype(jnp.bfloat16),
                        values[:, lanes],
                        preferred_element_type=jnp.float32,
                    )
                    spot = pl.ds(pl.multiple_of(c * WIDE + h * HEAD, HEAD), HEAD)
                    attn[i * TILE : (i + 1) * TILE, spot] = (summed / total).astype(jnp.bfloat16)

        def do_heads(c, inner):
            @pl.when(beside_last)
            def _():
                first = 1 + c * per_chunk
                until = jnp.minimum(first + per_chunk, n_seq - 1)
                lax.fori_loop(first, until, forward_last, 0)

            ahead = jnp.minimum(c, CHUNKS - 1)
            project(ahead)
            attend(jnp.maximum(c - 1, 0))
            keep(ahead)
            return inner

        lax.fori_loop(0, CHUNKS + 1, do_heads, 0)

        pl.when(beside_last)(finish_last)

        def do_out(c, inner):
            columns = pl.ds(pl.multiple_of(c * WIDE, WIDE), WIDE)
            mixed = jnp.dot(attn[...], weights[c, 3], preferred_element_type=jnp.float32)
            entering = xbuf[patch, 1, :, columns].astype(jnp.float32)
            out_ref[patch, :, columns] = (entering + mixed).astype(jnp.bfloat16)
            return inner

        lax.fori_loop(0, CHUNKS, do_out, 0)

        @pl.when(has_next)
        def _():
            pl.when(has_left)(lambda: x_copy(out_ref, patch, -1, seg + 1).start())
            pl.when(has_right)(lambda: x_copy(out_ref, patch, 1, seg + 1).start())
            x_copy(out_ref, patch, 0, seg + 1).start()

        return carry

    def latent_left(patch, carry):
        pl.when(has_left)(lambda: x_copy(latent_ref, patch, -1, seg).wait_send())
        pl.when(has_right)(lambda: x_copy(latent_ref, patch, 1, seg).wait_send())
        return carry

    @pl.when(seg == 0)
    def _():
        lax.fori_loop(0, PATCHES, latent_left, 0)

    lax.fori_loop(0, PATCHES, do_patch, 0)

    def drain_ring(step, carry):
        for part, way in parts:
            ring_copy(step, way, part).wait_send()
        for way in range(2):
            last_copy(step, way).wait_send()
        return carry

    lax.fori_loop(0, n_seq - 1, drain_ring, 0)
    pl.when(has_left)(lambda: stale_copy(-1).wait_send())
    pl.when(has_right)(lambda: stale_copy(1).wait_send())

    def drain_x(patch, carry):
        x_copy(out_ref, patch, 0, seg + 1).wait_send()
        pl.when(has_left)(lambda: x_copy(out_ref, patch, -1, seg + 1).wait_send())
        pl.when(has_right)(lambda: x_copy(out_ref, patch, 1, seg + 1).wait_send())
        return carry

    @pl.when(has_next)
    def _():
        lax.fori_loop(0, PATCHES, drain_x, 0)


def per_device(
    n_seg,
    n_seq,
    latent,
    stale_kv,
    query_weight,
    key_weight,
    value_weight,
    out_weight,
    query_gain,
    key_gain,
    tile_mask,
):
    tok_dev = latent.shape[0]
    patch_rows = tok_dev // PATCHES
    tiles_dev = tile_mask.shape[0]
    seq = lax.axis_index("seq")
    usable = tile_mask >= 0
    own = tiles_dev + jnp.arange(tiles_dev, dtype=jnp.int32)[:, None]
    tidx = jnp.where(usable, tile_mask - (seq - 1) * tiles_dev, own)
    listed = jnp.repeat(usable, TILE, axis=1).astype(jnp.float32)[:, None, :]
    vmem = pl.BlockSpec(memory_space=pltpu.VMEM)
    smem = pl.BlockSpec(memory_space=pltpu.SMEM)
    anywhere = pl.BlockSpec(memory_space=pl.ANY)
    steps = n_seq - 1
    dma = pltpu.SemaphoreType.DMA
    result = pl.pallas_call(
        functools.partial(kernel, n_seg, n_seq),
        out_shape=jax.ShapeDtypeStruct((PATCHES, patch_rows, D), jnp.bfloat16),
        in_specs=[smem, vmem, vmem, vmem, vmem] + [anywhere] * 5,
        out_specs=vmem,
        scratch_shapes=[
            pltpu.VMEM((CHUNKS, MATS, D, WIDE), jnp.bfloat16),
            pltpu.VMEM((2, 3 * tiles_dev, TILE, D), jnp.bfloat16),
            pltpu.VMEM((PATCHES, 3, patch_rows, D), jnp.bfloat16),
            pltpu.VMEM((patch_rows, D), jnp.bfloat16),
            pltpu.VMEM((patch_rows, WIDE), jnp.bfloat16),
            pltpu.VMEM((patch_rows, WIDE), jnp.bfloat16),
            pltpu.VMEM((2, 3 * patch_rows, WIDE), jnp.bfloat16),
            dma((MATS * CHUNKS,)),
            dma,
            dma((2, steps, LANE_CHUNKS)),
            dma((2, steps, LANE_CHUNKS)),
            dma((2, steps)),
            dma((2, steps)),
            pltpu.SemaphoreType.REGULAR,
            dma((3,)),
            dma((3,)),
            dma((PATCHES, 3)),
            dma((PATCHES, 3)),
        ],
        compiler_params=pltpu.CompilerParams(
            collective_id=0, has_side_effects=True, vmem_limit_bytes=56 * 1024 * 1024
        ),
    )(
        tidx,
        listed,
        query_gain,
        key_gain,
        latent.reshape(PATCHES, patch_rows, D),
        stale_kv[0].reshape(2, tiles_dev, TILE, D),
        query_weight[0],
        key_weight[0],
        value_weight[0],
        out_weight[0],
    )
    return result.reshape(1, tok_dev, D)


def solution(mesh):
    return jax.shard_map(
        functools.partial(per_device, mesh.shape["segment"], mesh.shape["seq"]),
        mesh=mesh,
        in_specs=(
            P("seq", None),
            P("segment", None, "seq", None),
            P("segment", "seq", None),
            P("segment", "seq", None),
            P("segment", "seq", None),
            P("segment", "seq", None),
            P("segment", None),
            P("segment", None),
            P("seq", None),
        ),
        out_specs=P("segment", "seq", None),
        check_vma=False,
    )
```

```python
import functools
import math

import jax
import jax.numpy as jnp
from jax import lax
from jax.experimental import pallas as pl
from jax.experimental.pallas import tpu as pltpu
from jax.sharding import PartitionSpec as P

D = 1536
HEADS = 12
HEAD = 128
TILE = 64
PATCHES = 3
TPP = 2
TPD = PATCHES * TPP
WIDE = 256
CHUNKS = D // WIDE
LANE_CHUNKS = CHUNKS // 2
MATS = 4
EPSILON = 1e-06
MESH = pl.DeviceIdType.MESH


def head_normed(projected, gain):
    mean = jnp.mean(projected * projected, axis=-1, keepdims=True)
    return (projected * lax.rsqrt(mean + EPSILON) * gain).astype(jnp.bfloat16)


def ring_place(seq, n):
    half = seq // 2
    return jnp.where(seq % 2 == 0, half, n - 1 - half)


def ring_seq(place, n):
    return jnp.where(place < n // 2, 2 * place, 2 * (n - 1 - place) + 1)


def kernel(
    n_seg,
    n_seq,
    tidx_ref,
    listed_ref,
    gain_q_ref,
    gain_k_ref,
    latent_ref,
    stale_ref,
    wq_ref,
    wk_ref,
    wv_ref,
    wo_ref,
    out_ref,
    weights,
    kv,
    xbuf,
    attn,
    queries,
    fresh_q,
    fresh,
    load_sem,
    own_sem,
    ring_send,
    ring_recv,
    last_send,
    last_recv,
    go_sem,
    stale_send,
    stale_recv,
    x_send,
    x_recv,
):
    seg = lax.axis_index("segment")
    seq = lax.axis_index("seq")
    depth = wq_ref.shape[0]
    patch_rows = xbuf.shape[2]
    has_left = seq > 0
    has_right = seq < n_seq - 1
    has_next = seg < n_seg - 1
    has_prev = seg > 0
    place = ring_place(seq, n_seq)
    ring_right = ring_seq(lax.rem(place + 1, n_seq), n_seq)
    ring_left = ring_seq(lax.rem(place + n_seq - 1, n_seq), n_seq)

    mine = pl.ds(pl.multiple_of(seq * depth, 16), depth)
    loads = []
    for mat, ref in enumerate((wq_ref, wk_ref, wv_ref, wo_ref)):
        for c in range(CHUNKS):
            loads.append(
                pltpu.make_async_copy(
                    ref.at[:, pl.ds(c * WIDE, WIDE)],
                    weights.at[c, mat, mine, :],
                    load_sem.at[mat * CHUNKS + c],
                )
            )
    for load in loads:
        load.start()
    own_stale = pltpu.make_async_copy(
        stale_ref.at[:, pl.ds(TPP, TPD - TPP)],
        kv.at[:, pl.ds(TPD + TPP, TPD - TPP)],
        own_sem,
    )
    own_stale.start()

    @pl.when(jnp.logical_not(has_left))
    def _():
        xbuf[:, 0] = jnp.zeros((PATCHES, patch_rows, D), jnp.bfloat16)

    @pl.when(jnp.logical_not(has_right))
    def _():
        xbuf[:, 2] = jnp.zeros((PATCHES, patch_rows, D), jnp.bfloat16)

    @pl.when(seg == 0)
    def _():
        xbuf[:, 1] = latent_ref[...]

    barrier = pltpu.get_barrier_semaphore()
    sides = ((-1, has_left), (0, None), (1, has_right))

    def greet(to_seg, to_seq):
        pl.semaphore_signal(barrier, inc=1, device_id=(to_seg, to_seq), device_id_type=MESH)

    greet(seg, ring_right)
    greet(seg, ring_left)
    pl.when(has_left)(lambda: greet(seg, seq - 1))
    pl.when(has_right)(lambda: greet(seg, seq + 1))
    for by, there in sides:
        ahead = has_next if there is None else jnp.logical_and(has_next, there)
        behind = has_prev if there is None else jnp.logical_and(has_prev, there)
        pl.when(ahead)(functools.partial(greet, seg + 1, seq + by))
        pl.when(behind)(functools.partial(greet, seg - 1, seq + by))
    beside = has_left.astype(jnp.int32) + has_right.astype(jnp.int32)
    levels = has_next.astype(jnp.int32) + has_prev.astype(jnp.int32)
    two_left = seq >= 2
    two_right = seq < n_seq - 2
    pl.when(two_left)(lambda: greet(seg, seq - 2))
    pl.when(two_right)(lambda: greet(seg, seq + 2))
    farther = two_left.astype(jnp.int32) + two_right.astype(jnp.int32)
    pl.semaphore_wait(barrier, 2 + beside + farther + levels * (1 + beside))

    def x_copy(src, patch, by, to_seg):
        return pltpu.make_async_remote_copy(
            src_ref=src.at[patch],
            dst_ref=xbuf.at[patch, 1 - by],
            send_sem=x_send.at[patch, 1 - by],
            recv_sem=x_recv.at[patch, 1 - by],
            device_id=(to_seg, seq + by),
            device_id_type=MESH,
        )

    toward = jnp.where(lax.rem(seq, 2) == 0, 1, -1)
    hands_on = jnp.logical_and(seq + 2 * toward >= 0, seq + 2 * toward < n_seq)
    is_handed = jnp.logical_and(seq - 2 * toward >= 0, seq - 2 * toward < n_seq)

    def stale_rows(slot):
        return kv.at[:, pl.ds(slot * TPD + TPP, TPD - TPP)]

    def stale_copy(landing=None):
        landing = 1 - toward if landing is None else landing
        return pltpu.make_async_remote_copy(
            src_ref=stale_ref.at[:, pl.ds(TPP, TPD - TPP)],
            dst_ref=stale_rows(landing),
            send_sem=stale_send.at[0],
            recv_sem=stale_recv.at[0],
            device_id=(seg, seq + toward),
            device_id_type=MESH,
        )

    def stale_handed():
        return pltpu.make_async_remote_copy(
            src_ref=stale_rows(1 + toward),
            dst_ref=stale_rows(1 - toward),
            send_sem=stale_send.at[1],
            recv_sem=stale_recv.at[1],
            device_id=(seg, seq + 2 * toward),
            device_id_type=MESH,
        )

    def ring_send_to(way, block, send_sem, recv_sem):
        return pltpu.make_async_remote_copy(
            src_ref=block,
            dst_ref=block,
            send_sem=send_sem,
            recv_sem=recv_sem,
            device_id=(seg, ring_right if way == 0 else ring_left),
            device_id_type=MESH,
        )

    def ring_rows(step, way, late):
        owner = lax.rem(place + (n_seq - step - late if way == 0 else step + late), n_seq)
        return pl.ds(pl.multiple_of(ring_seq(owner, n_seq) * depth, 16), depth)

    def ring_copy(step, way, part, late=0):
        rows = ring_rows(step, way, late)
        block = weights.at[way * LANE_CHUNKS + part, pl.ds(0, MATS - 1), rows, :]
        return ring_send_to(way, block, ring_send.at[way, step, part], ring_recv.at[way, step, part])

    def last_copy(step, way, late=0):
        rows = ring_rows(step, way, late)
        block = weights.at[pl.ds(way * LANE_CHUNKS, LANE_CHUNKS), MATS - 1, rows, :]
        return ring_send_to(way, block, last_send.at[way, step], last_recv.at[way, step])

    parts = [(part, way) for part in range(LANE_CHUNKS) for way in range(2)]
    odd = lax.rem(seg, 2) == 1
    for load in loads:
        load.wait()

    def send_latent(patch, carry):
        pl.when(has_left)(lambda: x_copy(latent_ref, patch, -1, seg).start())
        pl.when(has_right)(lambda: x_copy(latent_ref, patch, 1, seg).start())
        return carry

    @pl.when(seg == 0)
    def _():
        lax.fori_loop(0, PATCHES, send_latent, 0)

    pl.when(odd)(lambda: pl.semaphore_wait(go_sem, 1))
    for part, way in parts:
        ring_copy(0, way, part).start()
    stale_copy().start()

    def forward(step, carry):
        for part, way in parts:
            ring_copy(step - 1, way, part, 1).wait_recv()
            ring_copy(step, way, part).start()

        @pl.when(jnp.logical_and(step == n_seq // 2 - 1, jnp.logical_not(odd)))
        def _():
            pl.semaphore_signal(go_sem, inc=1, device_id=(seg + 1, seq), device_id_type=MESH)

        @pl.when(step == n_seq // 2 - 1)
        def _():
            stale_copy(1 + toward).wait_recv()
            pl.when(hands_on)(lambda: stale_handed().start())

        return carry

    lax.fori_loop(1, n_seq - 1, forward, 0)
    for way in range(2):
        last_copy(0, way).start()
    for part, way in parts:
        ring_copy(n_seq - 2, way, part, 1).wait_recv()

    def forward_last(step, carry):
        for way in range(2):
            last_copy(step - 1, way, 1).wait_recv()
            last_copy(step, way).start()
        return carry

    def finish_last():
        for way in range(2):
            last_copy(n_seq - 2, way, 1).wait_recv()

    early = seg < 2
    per_chunk = pl.cdiv(n_seq - 2, CHUNKS)

    @pl.when(jnp.logical_not(early))
    def _():
        lax.fori_loop(1, n_seq - 1, forward_last, 0)
        finish_last()

    own_stale.wait()
    pl.when(is_handed)(lambda: stale_handed().wait_recv())
    pl.when(hands_on)(lambda: stale_handed().wait_send())

    gain_q = gain_q_ref[...]
    gain_k = gain_k_ref[...]

    def do_patch(patch, carry):
        pl.when(has_left)(lambda: x_copy(out_ref, patch, 1, seg).wait_recv())
        pl.when(has_right)(lambda: x_copy(out_ref, patch, -1, seg).wait_recv())
        pl.when(has_prev)(lambda: x_copy(out_ref, patch, 0, seg).wait_recv())

        beside_last = jnp.logical_and(early, patch == 0)

        def project(c):
            rows3 = xbuf[patch].reshape(3 * patch_rows, D)
            k = jnp.dot(rows3, weights[c, 1], preferred_element_type=jnp.float32)
            for h in range(WIDE // HEAD):
                lanes = slice(h * HEAD, (h + 1) * HEAD)
                fresh[0, :, lanes] = head_normed(k[:, lanes], gain_k)
            v = jnp.dot(rows3, weights[c, 2], preferred_element_type=jnp.float32)
            fresh[1] = v.astype(jnp.bfloat16)
            q = jnp.dot(xbuf[patch, 1], weights[c, 0], preferred_element_type=jnp.float32)
            for h in range(WIDE // HEAD):
                lanes = slice(h * HEAD, (h + 1) * HEAD)
                fresh_q[:, lanes] = head_normed(q[:, lanes], gain_q)

        def keep(c):
            columns = pl.ds(pl.multiple_of(c * WIDE, WIDE), WIDE)
            queries[...] = fresh_q[...]
            for f in range(3):
                tiles = pl.ds(f * TPD + patch * TPP, TPP)
                rows = slice(f * patch_rows, (f + 1) * patch_rows)
                for which in range(2):
                    kv[which, tiles, :, columns] = fresh[which, rows].reshape(TPP, TILE, WIDE)

        def attend(c):
            columns = pl.ds(pl.multiple_of(c * WIDE, WIDE), WIDE)
            for i in range(TPP):
                g = patch * TPP + i
                places = [tidx_ref[g, m] for m in range(TPD)]
                listed = listed_ref[g]
                keys = jnp.concatenate([kv[0, t, :, columns] for t in places], axis=0)
                values = jnp.concatenate([kv[1, t, :, columns] for t in places], axis=0)
                own = queries[i * TILE : (i + 1) * TILE, :]
                for h in range(WIDE // HEAD):
                    lanes = slice(h * HEAD, (h + 1) * HEAD)
                    score = lax.dot_general(
                        own[:, lanes],
                        keys[:, lanes],
                        (((1,), (1,)), ((), ())),
                        preferred_element_type=jnp.float32,
                    )
                    weight = jnp.exp(score * (1.0 / math.sqrt(HEAD))) * listed
                    total = jnp.sum(weight, axis=-1, keepdims=True)
                    summed = jnp.dot(
                        weight.astype(jnp.bfloat16),
                        values[:, lanes],
                        preferred_element_type=jnp.float32,
                    )
                    spot = pl.ds(pl.multiple_of(c * WIDE + h * HEAD, HEAD), HEAD)
                    attn[i * TILE : (i + 1) * TILE, spot] = (summed / total).astype(jnp.bfloat16)

        def do_heads(c, inner):
            @pl.when(beside_last)
            def _():
                first = 1 + c * per_chunk
                until = jnp.minimum(first + per_chunk, n_seq - 1)
                lax.fori_loop(first, until, forward_last, 0)

            ahead = jnp.minimum(c, CHUNKS - 1)
            project(ahead)
            attend(jnp.maximum(c - 1, 0))
            keep(ahead)
            return inner

        lax.fori_loop(0, CHUNKS + 1, do_heads, 0)

        pl.when(beside_last)(finish_last)

        def do_out(c, inner):
            columns = pl.ds(pl.multiple_of(c * WIDE, WIDE), WIDE)
            mixed = jnp.dot(attn[...], weights[c, 3], preferred_element_type=jnp.float32)
            entering = xbuf[patch, 1, :, columns].astype(jnp.float32)
            out_ref[patch, :, columns] = (entering + mixed).astype(jnp.bfloat16)
            return inner

        lax.fori_loop(0, CHUNKS, do_out, 0)

        @pl.when(has_next)
        def _():
            pl.when(has_left)(lambda: x_copy(out_ref, patch, -1, seg + 1).start())
            pl.when(has_right)(lambda: x_copy(out_ref, patch, 1, seg + 1).start())
            x_copy(out_ref, patch, 0, seg + 1).start()

        return carry

    def latent_left(patch, carry):
        pl.when(has_left)(lambda: x_copy(latent_ref, patch, -1, seg).wait_send())
        pl.when(has_right)(lambda: x_copy(latent_ref, patch, 1, seg).wait_send())
        return carry

    @pl.when(seg == 0)
    def _():
        lax.fori_loop(0, PATCHES, latent_left, 0)

    lax.fori_loop(0, PATCHES, do_patch, 0)

    def drain_ring(step, carry):
        for part, way in parts:
            ring_copy(step, way, part).wait_send()
        for way in range(2):
            last_copy(step, way).wait_send()
        return carry

    lax.fori_loop(0, n_seq - 1, drain_ring, 0)
    stale_copy().wait_send()

    def drain_x(patch, carry):
        x_copy(out_ref, patch, 0, seg + 1).wait_send()
        pl.when(has_left)(lambda: x_copy(out_ref, patch, -1, seg + 1).wait_send())
        pl.when(has_right)(lambda: x_copy(out_ref, patch, 1, seg + 1).wait_send())
        return carry

    @pl.when(has_next)
    def _():
        lax.fori_loop(0, PATCHES, drain_x, 0)


def per_device(
    n_seg,
    n_seq,
    latent,
    stale_kv,
    query_weight,
    key_weight,
    value_weight,
    out_weight,
    query_gain,
    key_gain,
    tile_mask,
):
    tok_dev = latent.shape[0]
    patch_rows = tok_dev // PATCHES
    tiles_dev = tile_mask.shape[0]
    seq = lax.axis_index("seq")
    usable = tile_mask >= 0
    own = tiles_dev + jnp.arange(tiles_dev, dtype=jnp.int32)[:, None]
    tidx = jnp.where(usable, tile_mask - (seq - 1) * tiles_dev, own)
    listed = jnp.repeat(usable, TILE, axis=1).astype(jnp.float32)[:, None, :]
    vmem = pl.BlockSpec(memory_space=pltpu.VMEM)
    smem = pl.BlockSpec(memory_space=pltpu.SMEM)
    anywhere = pl.BlockSpec(memory_space=pl.ANY)
    steps = n_seq - 1
    dma = pltpu.SemaphoreType.DMA
    result = pl.pallas_call(
        functools.partial(kernel, n_seg, n_seq),
        out_shape=jax.ShapeDtypeStruct((PATCHES, patch_rows, D), jnp.bfloat16),
        in_specs=[smem, vmem, vmem, vmem, vmem] + [anywhere] * 5,
        out_specs=vmem,
        scratch_shapes=[
            pltpu.VMEM((CHUNKS, MATS, D, WIDE), jnp.bfloat16),
            pltpu.VMEM((2, 3 * tiles_dev, TILE, D), jnp.bfloat16),
            pltpu.VMEM((PATCHES, 3, patch_rows, D), jnp.bfloat16),
            pltpu.VMEM((patch_rows, D), jnp.bfloat16),
            pltpu.VMEM((patch_rows, WIDE), jnp.bfloat16),
            pltpu.VMEM((patch_rows, WIDE), jnp.bfloat16),
            pltpu.VMEM((2, 3 * patch_rows, WIDE), jnp.bfloat16),
            dma((MATS * CHUNKS,)),
            dma,
            dma((2, steps, LANE_CHUNKS)),
            dma((2, steps, LANE_CHUNKS)),
            dma((2, steps)),
            dma((2, steps)),
            pltpu.SemaphoreType.REGULAR,
            dma((2,)),
            dma((2,)),
            dma((PATCHES, 3)),
            dma((PATCHES, 3)),
        ],
        compiler_params=pltpu.CompilerParams(
            collective_id=0, has_side_effects=True, vmem_limit_bytes=56 * 1024 * 1024
        ),
    )(
        tidx,
        listed,
        query_gain,
        key_gain,
        latent.reshape(PATCHES, patch_rows, D),
        stale_kv[0].reshape(2, tiles_dev, TILE, D),
        query_weight[0],
        key_weight[0],
        value_weight[0],
        out_weight[0],
    )
    return result.reshape(1, tok_dev, D)


def solution(mesh):
    return jax.shard_map(
        functools.partial(per_device, mesh.shape["segment"], mesh.shape["seq"]),
        mesh=mesh,
        in_specs=(
            P("seq", None),
            P("segment", None, "seq", None),
            P("segment", "seq", None),
            P("segment", "seq", None),
            P("segment", "seq", None),
            P("segment", "seq", None),
            P("segment", None),
            P("segment", None),
            P("seq", None),
        ),
        out_specs=P("segment", "seq", None),
        check_vma=False,
    )
```

```python
import functools
import math

import jax
import jax.numpy as jnp
from jax import lax
from jax.experimental import pallas as pl
from jax.experimental.pallas import tpu as pltpu
from jax.sharding import PartitionSpec as P

D = 1536
HEADS = 12
HEAD = 128
TILE = 64
PATCHES = 3
TPP = 2
TPD = PATCHES * TPP
WIDE = 256
CHUNKS = D // WIDE
LANE_CHUNKS = CHUNKS // 2
MATS = 4
EPSILON = 1e-06
MESH = pl.DeviceIdType.MESH


def head_normed(projected, gain):
    mean = jnp.mean(projected * projected, axis=-1, keepdims=True)
    return (projected * lax.rsqrt(mean + EPSILON) * gain).astype(jnp.bfloat16)


def ring_place(seq, n):
    half = seq // 2
    return jnp.where(seq % 2 == 0, half, n - 1 - half)


def ring_seq(place, n):
    return jnp.where(place < n // 2, 2 * place, 2 * (n - 1 - place) + 1)


def kernel(
    n_seg,
    n_seq,
    tidx_ref,
    listed_ref,
    gain_q_ref,
    gain_k_ref,
    latent_ref,
    stale_ref,
    wq_ref,
    wk_ref,
    wv_ref,
    wo_ref,
    out_ref,
    weights,
    kv,
    xbuf,
    attn,
    queries,
    fresh_q,
    fresh,
    load_sem,
    own_sem,
    ring_send,
    ring_recv,
    last_send,
    last_recv,
    go_sem,
    stale_send,
    stale_recv,
    x_send,
    x_recv,
):
    seg = lax.axis_index("segment")
    seq = lax.axis_index("seq")
    depth = wq_ref.shape[0]
    patch_rows = xbuf.shape[2]
    has_left = seq > 0
    has_right = seq < n_seq - 1
    has_next = seg < n_seg - 1
    has_prev = seg > 0
    place = ring_place(seq, n_seq)
    ring_right = ring_seq(lax.rem(place + 1, n_seq), n_seq)
    ring_left = ring_seq(lax.rem(place + n_seq - 1, n_seq), n_seq)

    mine = pl.ds(pl.multiple_of(seq * depth, 16), depth)
    loads = []
    for mat, ref in enumerate((wq_ref, wk_ref, wv_ref, wo_ref)):
        for c in range(CHUNKS):
            loads.append(
                pltpu.make_async_copy(
                    ref.at[:, pl.ds(c * WIDE, WIDE)],
                    weights.at[c, mat, mine, :],
                    load_sem.at[mat * CHUNKS + c],
                )
            )
    for load in loads:
        load.start()
    own_stale = pltpu.make_async_copy(
        stale_ref.at[:, pl.ds(TPP, TPD - TPP)],
        kv.at[:, pl.ds(TPD + TPP, TPD - TPP)],
        own_sem,
    )
    own_stale.start()

    @pl.when(jnp.logical_not(has_left))
    def _():
        xbuf[:, 0] = jnp.zeros((PATCHES, patch_rows, D), jnp.bfloat16)

    @pl.when(jnp.logical_not(has_right))
    def _():
        xbuf[:, 2] = jnp.zeros((PATCHES, patch_rows, D), jnp.bfloat16)

    @pl.when(seg == 0)
    def _():
        xbuf[:, 1] = latent_ref[...]

    barrier = pltpu.get_barrier_semaphore()
    sides = ((-1, has_left), (0, None), (1, has_right))

    def greet(to_seg, to_seq):
        pl.semaphore_signal(barrier, inc=1, device_id=(to_seg, to_seq), device_id_type=MESH)

    greet(seg, ring_right)
    greet(seg, ring_left)
    pl.when(has_left)(lambda: greet(seg, seq - 1))
    pl.when(has_right)(lambda: greet(seg, seq + 1))
    for by, there in sides:
        ahead = has_next if there is None else jnp.logical_and(has_next, there)
        behind = has_prev if there is None else jnp.logical_and(has_prev, there)
        pl.when(ahead)(functools.partial(greet, seg + 1, seq + by))
        pl.when(behind)(functools.partial(greet, seg - 1, seq + by))
    beside = has_left.astype(jnp.int32) + has_right.astype(jnp.int32)
    levels = has_next.astype(jnp.int32) + has_prev.astype(jnp.int32)
    two_left = seq >= 2
    two_right = seq < n_seq - 2
    pl.when(two_left)(lambda: greet(seg, seq - 2))
    pl.when(two_right)(lambda: greet(seg, seq + 2))
    farther = two_left.astype(jnp.int32) + two_right.astype(jnp.int32)
    pl.semaphore_wait(barrier, 2 + beside + farther + levels * (1 + beside))

    def x_copy(src, patch, by, to_seg):
        return pltpu.make_async_remote_copy(
            src_ref=src.at[patch],
            dst_ref=xbuf.at[patch, 1 - by],
            send_sem=x_send.at[patch, 1 - by],
            recv_sem=x_recv.at[patch, 1 - by],
            device_id=(to_seg, seq + by),
            device_id_type=MESH,
        )

    toward = jnp.where(lax.rem(seq, 2) == 0, 1, -1)
    hands_on = jnp.logical_and(seq + 2 * toward >= 0, seq + 2 * toward < n_seq)
    is_handed = jnp.logical_and(seq - 2 * toward >= 0, seq - 2 * toward < n_seq)

    def stale_rows(slot):
        return kv.at[:, pl.ds(slot * TPD + TPP, TPD - TPP)]

    def stale_copy(landing=None):
        landing = 1 - toward if landing is None else landing
        return pltpu.make_async_remote_copy(
            src_ref=stale_ref.at[:, pl.ds(TPP, TPD - TPP)],
            dst_ref=stale_rows(landing),
            send_sem=stale_send.at[0],
            recv_sem=stale_recv.at[0],
            device_id=(seg, seq + toward),
            device_id_type=MESH,
        )

    def stale_handed():
        return pltpu.make_async_remote_copy(
            src_ref=stale_rows(1 + toward),
            dst_ref=stale_rows(1 - toward),
            send_sem=stale_send.at[1],
            recv_sem=stale_recv.at[1],
            device_id=(seg, seq + 2 * toward),
            device_id_type=MESH,
        )

    def ring_send_to(way, block, send_sem, recv_sem):
        return pltpu.make_async_remote_copy(
            src_ref=block,
            dst_ref=block,
            send_sem=send_sem,
            recv_sem=recv_sem,
            device_id=(seg, ring_right if way == 0 else ring_left),
            device_id_type=MESH,
        )

    def ring_rows(step, way, late):
        owner = lax.rem(place + (n_seq - step - late if way == 0 else step + late), n_seq)
        return pl.ds(pl.multiple_of(ring_seq(owner, n_seq) * depth, 16), depth)

    def ring_copy(step, way, part, late=0):
        rows = ring_rows(step, way, late)
        block = weights.at[way * LANE_CHUNKS + part, pl.ds(0, MATS - 1), rows, :]
        return ring_send_to(way, block, ring_send.at[way, step, part], ring_recv.at[way, step, part])

    def last_copy(step, way, late=0):
        rows = ring_rows(step, way, late)
        block = weights.at[pl.ds(way * LANE_CHUNKS, LANE_CHUNKS), MATS - 1, rows, :]
        return ring_send_to(way, block, last_send.at[way, step], last_recv.at[way, step])

    parts = [(part, way) for part in range(LANE_CHUNKS) for way in range(2)]
    odd = lax.rem(seg, 2) == 1
    for load in loads:
        load.wait()

    def latent_handed(patch):
        return pltpu.make_async_remote_copy(
            src_ref=xbuf.at[patch, 1 + toward],
            dst_ref=xbuf.at[patch, 1 - toward],
            send_sem=x_send.at[patch, 1 + toward],
            recv_sem=x_recv.at[patch, 1 - toward],
            device_id=(seg, seq + 2 * toward),
            device_id_type=MESH,
        )

    def send_latent(patch, carry):
        x_copy(latent_ref, patch, toward, seg).start()
        return carry

    def hand_latent(patch, carry):
        x_copy(latent_ref, patch, -toward, seg).wait_recv()
        pl.when(hands_on)(lambda: latent_handed(patch).start())
        return carry

    @pl.when(seg == 0)
    def _():
        lax.fori_loop(0, PATCHES, send_latent, 0)

    pl.when(odd)(lambda: pl.semaphore_wait(go_sem, 1))
    for part, way in parts:
        ring_copy(0, way, part).start()
    stale_copy().start()

    def forward(step, carry):
        for part, way in parts:
            ring_copy(step - 1, way, part, 1).wait_recv()
            ring_copy(step, way, part).start()

        @pl.when(jnp.logical_and(step == n_seq // 2 - 1, jnp.logical_not(odd)))
        def _():
            pl.semaphore_signal(go_sem, inc=1, device_id=(seg + 1, seq), device_id_type=MESH)

        @pl.when(step == n_seq // 2 - 1)
        def _():
            stale_copy(1 + toward).wait_recv()
            pl.when(hands_on)(lambda: stale_handed().start())

            @pl.when(seg == 0)
            def _():
                lax.fori_loop(0, PATCHES, hand_latent, 0)

        return carry

    lax.fori_loop(1, n_seq - 1, forward, 0)
    for way in range(2):
        last_copy(0, way).start()
    for part, way in parts:
        ring_copy(n_seq - 2, way, part, 1).wait_recv()

    def forward_last(step, carry):
        for way in range(2):
            last_copy(step - 1, way, 1).wait_recv()
            last_copy(step, way).start()
        return carry

    def finish_last():
        for way in range(2):
            last_copy(n_seq - 2, way, 1).wait_recv()

    early = seg < 2
    per_chunk = pl.cdiv(n_seq - 2, CHUNKS)

    @pl.when(jnp.logical_not(early))
    def _():
        lax.fori_loop(1, n_seq - 1, forward_last, 0)
        finish_last()

    own_stale.wait()
    pl.when(is_handed)(lambda: stale_handed().wait_recv())
    pl.when(hands_on)(lambda: stale_handed().wait_send())

    gain_q = gain_q_ref[...]
    gain_k = gain_k_ref[...]

    waits_left = jnp.logical_and(has_left, jnp.logical_or(has_prev, toward == 1))
    waits_right = jnp.logical_and(has_right, jnp.logical_or(has_prev, toward == -1))

    def do_patch(patch, carry):
        pl.when(waits_left)(lambda: x_copy(out_ref, patch, 1, seg).wait_recv())
        pl.when(waits_right)(lambda: x_copy(out_ref, patch, -1, seg).wait_recv())
        pl.when(has_prev)(lambda: x_copy(out_ref, patch, 0, seg).wait_recv())

        beside_last = jnp.logical_and(early, patch == 0)

        def project(c):
            rows3 = xbuf[patch].reshape(3 * patch_rows, D)
            k = jnp.dot(rows3, weights[c, 1], preferred_element_type=jnp.float32)
            for h in range(WIDE // HEAD):
                lanes = slice(h * HEAD, (h + 1) * HEAD)
                fresh[0, :, lanes] = head_normed(k[:, lanes], gain_k)
            v = jnp.dot(rows3, weights[c, 2], preferred_element_type=jnp.float32)
            fresh[1] = v.astype(jnp.bfloat16)
            q = jnp.dot(xbuf[patch, 1], weights[c, 0], preferred_element_type=jnp.float32)
            for h in range(WIDE // HEAD):
                lanes = slice(h * HEAD, (h + 1) * HEAD)
                fresh_q[:, lanes] = head_normed(q[:, lanes], gain_q)

        def keep(c):
            columns = pl.ds(pl.multiple_of(c * WIDE, WIDE), WIDE)
            queries[...] = fresh_q[...]
            for f in range(3):
                tiles = pl.ds(f * TPD + patch * TPP, TPP)
                rows = slice(f * patch_rows, (f + 1) * patch_rows)
                for which in range(2):
                    kv[which, tiles, :, columns] = fresh[which, rows].reshape(TPP, TILE, WIDE)

        def attend(c):
            columns = pl.ds(pl.multiple_of(c * WIDE, WIDE), WIDE)
            for i in range(TPP):
                g = patch * TPP + i
                places = [tidx_ref[g, m] for m in range(TPD)]
                listed = listed_ref[g]
                keys = jnp.concatenate([kv[0, t, :, columns] for t in places], axis=0)
                values = jnp.concatenate([kv[1, t, :, columns] for t in places], axis=0)
                own = queries[i * TILE : (i + 1) * TILE, :]
                for h in range(WIDE // HEAD):
                    lanes = slice(h * HEAD, (h + 1) * HEAD)
                    score = lax.dot_general(
                        own[:, lanes],
                        keys[:, lanes],
                        (((1,), (1,)), ((), ())),
                        preferred_element_type=jnp.float32,
                    )
                    weight = jnp.exp(score * (1.0 / math.sqrt(HEAD))) * listed
                    total = jnp.sum(weight, axis=-1, keepdims=True)
                    summed = jnp.dot(
                        weight.astype(jnp.bfloat16),
                        values[:, lanes],
                        preferred_element_type=jnp.float32,
                    )
                    spot = pl.ds(pl.multiple_of(c * WIDE + h * HEAD, HEAD), HEAD)
                    attn[i * TILE : (i + 1) * TILE, spot] = (summed / total).astype(jnp.bfloat16)

        def do_heads(c, inner):
            @pl.when(beside_last)
            def _():
                first = 1 + c * per_chunk
                until = jnp.minimum(first + per_chunk, n_seq - 1)
                lax.fori_loop(first, until, forward_last, 0)

            ahead = jnp.minimum(c, CHUNKS - 1)
            project(ahead)
            attend(jnp.maximum(c - 1, 0))
            keep(ahead)
            return inner

        lax.fori_loop(0, CHUNKS + 1, do_heads, 0)

        pl.when(beside_last)(finish_last)

        def do_out(c, inner):
            columns = pl.ds(pl.multiple_of(c * WIDE, WIDE), WIDE)
            mixed = jnp.dot(attn[...], weights[c, 3], preferred_element_type=jnp.float32)
            entering = xbuf[patch, 1, :, columns].astype(jnp.float32)
            out_ref[patch, :, columns] = (entering + mixed).astype(jnp.bfloat16)
            return inner

        lax.fori_loop(0, CHUNKS, do_out, 0)

        @pl.when(has_next)
        def _():
            pl.when(has_left)(lambda: x_copy(out_ref, patch, -1, seg + 1).start())
            pl.when(has_right)(lambda: x_copy(out_ref, patch, 1, seg + 1).start())
            x_copy(out_ref, patch, 0, seg + 1).start()

        return carry

    def latent_left(patch, carry):
        x_copy(latent_ref, patch, toward, seg).wait_send()
        pl.when(hands_on)(lambda: latent_handed(patch).wait_send())
        return carry

    @pl.when(seg == 0)
    def _():
        lax.fori_loop(0, PATCHES, latent_left, 0)

    lax.fori_loop(0, PATCHES, do_patch, 0)

    def drain_ring(step, carry):
        for part, way in parts:
            ring_copy(step, way, part).wait_send()
        for way in range(2):
            last_copy(step, way).wait_send()
        return carry

    lax.fori_loop(0, n_seq - 1, drain_ring, 0)
    stale_copy().wait_send()

    def drain_x(patch, carry):
        x_copy(out_ref, patch, 0, seg + 1).wait_send()
        pl.when(has_left)(lambda: x_copy(out_ref, patch, -1, seg + 1).wait_send())
        pl.when(has_right)(lambda: x_copy(out_ref, patch, 1, seg + 1).wait_send())
        return carry

    @pl.when(has_next)
    def _():
        lax.fori_loop(0, PATCHES, drain_x, 0)


def per_device(
    n_seg,
    n_seq,
    latent,
    stale_kv,
    query_weight,
    key_weight,
    value_weight,
    out_weight,
    query_gain,
    key_gain,
    tile_mask,
):
    tok_dev = latent.shape[0]
    patch_rows = tok_dev // PATCHES
    tiles_dev = tile_mask.shape[0]
    seq = lax.axis_index("seq")
    usable = tile_mask >= 0
    own = tiles_dev + jnp.arange(tiles_dev, dtype=jnp.int32)[:, None]
    tidx = jnp.where(usable, tile_mask - (seq - 1) * tiles_dev, own)
    listed = jnp.repeat(usable, TILE, axis=1).astype(jnp.float32)[:, None, :]
    vmem = pl.BlockSpec(memory_space=pltpu.VMEM)
    smem = pl.BlockSpec(memory_space=pltpu.SMEM)
    anywhere = pl.BlockSpec(memory_space=pl.ANY)
    steps = n_seq - 1
    dma = pltpu.SemaphoreType.DMA
    result = pl.pallas_call(
        functools.partial(kernel, n_seg, n_seq),
        out_shape=jax.ShapeDtypeStruct((PATCHES, patch_rows, D), jnp.bfloat16),
        in_specs=[smem, vmem, vmem, vmem, vmem] + [anywhere] * 5,
        out_specs=vmem,
        scratch_shapes=[
            pltpu.VMEM((CHUNKS, MATS, D, WIDE), jnp.bfloat16),
            pltpu.VMEM((2, 3 * tiles_dev, TILE, D), jnp.bfloat16),
            pltpu.VMEM((PATCHES, 3, patch_rows, D), jnp.bfloat16),
            pltpu.VMEM((patch_rows, D), jnp.bfloat16),
            pltpu.VMEM((patch_rows, WIDE), jnp.bfloat16),
            pltpu.VMEM((patch_rows, WIDE), jnp.bfloat16),
            pltpu.VMEM((2, 3 * patch_rows, WIDE), jnp.bfloat16),
            dma((MATS * CHUNKS,)),
            dma,
            dma((2, steps, LANE_CHUNKS)),
            dma((2, steps, LANE_CHUNKS)),
            dma((2, steps)),
            dma((2, steps)),
            pltpu.SemaphoreType.REGULAR,
            dma((2,)),
            dma((2,)),
            dma((PATCHES, 3)),
            dma((PATCHES, 3)),
        ],
        compiler_params=pltpu.CompilerParams(
            collective_id=0, has_side_effects=True, vmem_limit_bytes=56 * 1024 * 1024
        ),
    )(
        tidx,
        listed,
        query_gain,
        key_gain,
        latent.reshape(PATCHES, patch_rows, D),
        stale_kv[0].reshape(2, tiles_dev, TILE, D),
        query_weight[0],
        key_weight[0],
        value_weight[0],
        out_weight[0],
    )
    return result.reshape(1, tok_dev, D)


def solution(mesh):
    return jax.shard_map(
        functools.partial(per_device, mesh.shape["segment"], mesh.shape["seq"]),
        mesh=mesh,
        in_specs=(
            P("seq", None),
            P("segment", None, "seq", None),
            P("segment", "seq", None),
            P("segment", "seq", None),
            P("segment", "seq", None),
            P("segment", "seq", None),
            P("segment", None),
            P("segment", None),
            P("seq", None),
        ),
        out_specs=P("segment", "seq", None),
        check_vma=False,
    )
```

```python
import functools
import math

import jax
import jax.numpy as jnp
from jax import lax
from jax.experimental import pallas as pl
from jax.experimental.pallas import tpu as pltpu
from jax.sharding import PartitionSpec as P

D = 1536
HEADS = 12
HEAD = 128
TILE = 64
PATCHES = 3
TPP = 2
TPD = PATCHES * TPP
WIDE = 256
CHUNKS = D // WIDE
LANE_CHUNKS = CHUNKS // 2
MATS = 4
EPSILON = 1e-06
MESH = pl.DeviceIdType.MESH


def head_normed(projected, gain):
    mean = jnp.mean(projected * projected, axis=-1, keepdims=True)
    return (projected * lax.rsqrt(mean + EPSILON) * gain).astype(jnp.bfloat16)


def ring_place(seq, n):
    half = seq // 2
    return jnp.where(seq % 2 == 0, half, n - 1 - half)


def ring_seq(place, n):
    return jnp.where(place < n // 2, 2 * place, 2 * (n - 1 - place) + 1)


def kernel(
    n_seg,
    n_seq,
    tidx_ref,
    listed_ref,
    gain_q_ref,
    gain_k_ref,
    latent_ref,
    stale_ref,
    wq_ref,
    wk_ref,
    wv_ref,
    wo_ref,
    out_ref,
    weights,
    kv,
    xbuf,
    attn,
    queries,
    fresh_q,
    fresh,
    load_sem,
    own_sem,
    ring_send,
    ring_recv,
    last_send,
    last_recv,
    go_sem,
    stale_send,
    stale_recv,
    x_send,
    x_recv,
):
    seg = lax.axis_index("segment")
    seq = lax.axis_index("seq")
    depth = wq_ref.shape[0]
    patch_rows = xbuf.shape[2]
    has_left = seq > 0
    has_right = seq < n_seq - 1
    has_next = seg < n_seg - 1
    has_prev = seg > 0
    place = ring_place(seq, n_seq)
    ring_right = ring_seq(lax.rem(place + 1, n_seq), n_seq)
    ring_left = ring_seq(lax.rem(place + n_seq - 1, n_seq), n_seq)

    mine = pl.ds(pl.multiple_of(seq * depth, 16), depth)
    loads = []
    for mat, ref in enumerate((wq_ref, wk_ref, wv_ref, wo_ref)):
        for c in range(CHUNKS):
            loads.append(
                pltpu.make_async_copy(
                    ref.at[:, pl.ds(c * WIDE, WIDE)],
                    weights.at[c, mat, mine, :],
                    load_sem.at[mat * CHUNKS + c],
                )
            )
    for load in loads:
        load.start()
    own_stale = pltpu.make_async_copy(
        stale_ref.at[:, pl.ds(TPP, TPD - TPP)],
        kv.at[:, pl.ds(TPD + TPP, TPD - TPP)],
        own_sem,
    )
    own_stale.start()

    @pl.when(jnp.logical_not(has_left))
    def _():
        xbuf[:, 0] = jnp.zeros((PATCHES, patch_rows, D), jnp.bfloat16)

    @pl.when(jnp.logical_not(has_right))
    def _():
        xbuf[:, 2] = jnp.zeros((PATCHES, patch_rows, D), jnp.bfloat16)

    @pl.when(seg == 0)
    def _():
        xbuf[:, 1] = latent_ref[...]

    barrier = pltpu.get_barrier_semaphore()
    sides = ((-1, has_left), (0, None), (1, has_right))

    def greet(to_seg, to_seq):
        pl.semaphore_signal(barrier, inc=1, device_id=(to_seg, to_seq), device_id_type=MESH)

    greet(seg, ring_right)
    greet(seg, ring_left)
    pl.when(has_left)(lambda: greet(seg, seq - 1))
    pl.when(has_right)(lambda: greet(seg, seq + 1))
    for by, there in sides:
        ahead = has_next if there is None else jnp.logical_and(has_next, there)
        behind = has_prev if there is None else jnp.logical_and(has_prev, there)
        pl.when(ahead)(functools.partial(greet, seg + 1, seq + by))
        pl.when(behind)(functools.partial(greet, seg - 1, seq + by))
    beside = has_left.astype(jnp.int32) + has_right.astype(jnp.int32)
    levels = has_next.astype(jnp.int32) + has_prev.astype(jnp.int32)
    two_left = seq >= 2
    two_right = seq < n_seq - 2
    pl.when(two_left)(lambda: greet(seg, seq - 2))
    pl.when(two_right)(lambda: greet(seg, seq + 2))
    farther = two_left.astype(jnp.int32) + two_right.astype(jnp.int32)
    pl.semaphore_wait(barrier, 2 + beside + farther + levels * (1 + beside))

    def x_copy(src, patch, by, to_seg):
        return pltpu.make_async_remote_copy(
            src_ref=src.at[patch],
            dst_ref=xbuf.at[patch, 1 - by],
            send_sem=x_send.at[patch, 1 - by],
            recv_sem=x_recv.at[patch, 1 - by],
            device_id=(to_seg, seq + by),
            device_id_type=MESH,
        )

    toward = jnp.where(lax.rem(seq, 2) == 0, 1, -1)
    hands_on = jnp.logical_and(seq + 2 * toward >= 0, seq + 2 * toward < n_seq)
    is_handed = jnp.logical_and(seq - 2 * toward >= 0, seq - 2 * toward < n_seq)

    def stale_rows(slot):
        return kv.at[:, pl.ds(slot * TPD + TPP, TPD - TPP)]

    def stale_copy(landing=None):
        landing = 1 - toward if landing is None else landing
        return pltpu.make_async_remote_copy(
            src_ref=stale_ref.at[:, pl.ds(TPP, TPD - TPP)],
            dst_ref=stale_rows(landing),
            send_sem=stale_send.at[0],
            recv_sem=stale_recv.at[0],
            device_id=(seg, seq + toward),
            device_id_type=MESH,
        )

    def stale_handed():
        return pltpu.make_async_remote_copy(
            src_ref=stale_rows(1 + toward),
            dst_ref=stale_rows(1 - toward),
            send_sem=stale_send.at[1],
            recv_sem=stale_recv.at[1],
            device_id=(seg, seq + 2 * toward),
            device_id_type=MESH,
        )

    def ring_send_to(way, block, send_sem, recv_sem):
        return pltpu.make_async_remote_copy(
            src_ref=block,
            dst_ref=block,
            send_sem=send_sem,
            recv_sem=recv_sem,
            device_id=(seg, ring_right if way == 0 else ring_left),
            device_id_type=MESH,
        )

    def ring_rows(step, way, late):
        owner = lax.rem(place + (n_seq - step - late if way == 0 else step + late), n_seq)
        return pl.ds(pl.multiple_of(ring_seq(owner, n_seq) * depth, 16), depth)

    def ring_copy(step, way, part, late=0):
        rows = ring_rows(step, way, late)
        block = weights.at[way * LANE_CHUNKS + part, pl.ds(0, MATS - 1), rows, :]
        return ring_send_to(way, block, ring_send.at[way, step, part], ring_recv.at[way, step, part])

    def last_copy(step, way, late=0):
        rows = ring_rows(step, way, late)
        block = weights.at[pl.ds(way * LANE_CHUNKS, LANE_CHUNKS), MATS - 1, rows, :]
        return ring_send_to(way, block, last_send.at[way, step], last_recv.at[way, step])

    parts = [(part, way) for part in range(LANE_CHUNKS) for way in range(2)]
    odd = lax.rem(seg, 2) == 1
    for load in loads:
        load.wait()

    def send_latent(patch, carry):
        pl.when(has_left)(lambda: x_copy(latent_ref, patch, -1, seg).start())
        pl.when(has_right)(lambda: x_copy(latent_ref, patch, 1, seg).start())
        return carry

    @pl.when(seg == 0)
    def _():
        lax.fori_loop(0, PATCHES, send_latent, 0)

    pl.when(odd)(lambda: pl.semaphore_wait(go_sem, 1))
    for part, way in parts:
        ring_copy(0, way, part).start()
    stale_copy().start()

    def forward(step, carry):
        for part, way in parts:
            ring_copy(step - 1, way, part, 1).wait_recv()
            ring_copy(step, way, part).start()

        @pl.when(jnp.logical_and(step == 1, jnp.logical_not(odd)))
        def _():
            pl.semaphore_signal(go_sem, inc=1, device_id=(seg + 1, seq), device_id_type=MESH)

        @pl.when(step == n_seq // 2 - 1)
        def _():
            stale_copy(1 + toward).wait_recv()
            pl.when(hands_on)(lambda: stale_handed().start())

        return carry

    lax.fori_loop(1, n_seq - 1, forward, 0)
    for way in range(2):
        last_copy(0, way).start()
    for part, way in parts:
        ring_copy(n_seq - 2, way, part, 1).wait_recv()

    def forward_last(step, carry):
        for way in range(2):
            last_copy(step - 1, way, 1).wait_recv()
            last_copy(step, way).start()
        return carry

    def finish_last():
        for way in range(2):
            last_copy(n_seq - 2, way, 1).wait_recv()

    early = seg < 2
    per_chunk = pl.cdiv(n_seq - 2, CHUNKS)

    @pl.when(jnp.logical_not(early))
    def _():
        lax.fori_loop(1, n_seq - 1, forward_last, 0)
        finish_last()

    own_stale.wait()
    pl.when(is_handed)(lambda: stale_handed().wait_recv())
    pl.when(hands_on)(lambda: stale_handed().wait_send())

    gain_q = gain_q_ref[...]
    gain_k = gain_k_ref[...]

    def do_patch(patch, carry):
        pl.when(has_left)(lambda: x_copy(out_ref, patch, 1, seg).wait_recv())
        pl.when(has_right)(lambda: x_copy(out_ref, patch, -1, seg).wait_recv())
        pl.when(has_prev)(lambda: x_copy(out_ref, patch, 0, seg).wait_recv())

        beside_last = jnp.logical_and(early, patch == 0)

        def project(c):
            rows3 = xbuf[patch].reshape(3 * patch_rows, D)
            k = jnp.dot(rows3, weights[c, 1], preferred_element_type=jnp.float32)
            for h in range(WIDE // HEAD):
                lanes = slice(h * HEAD, (h + 1) * HEAD)
                fresh[0, :, lanes] = head_normed(k[:, lanes], gain_k)
            v = jnp.dot(rows3, weights[c, 2], preferred_element_type=jnp.float32)
            fresh[1] = v.astype(jnp.bfloat16)
            q = jnp.dot(xbuf[patch, 1], weights[c, 0], preferred_element_type=jnp.float32)
            for h in range(WIDE // HEAD):
                lanes = slice(h * HEAD, (h + 1) * HEAD)
                fresh_q[:, lanes] = head_normed(q[:, lanes], gain_q)

        def keep(c):
            columns = pl.ds(pl.multiple_of(c * WIDE, WIDE), WIDE)
            queries[...] = fresh_q[...]
            for f in range(3):
                tiles = pl.ds(f * TPD + patch * TPP, TPP)
                rows = slice(f * patch_rows, (f + 1) * patch_rows)
                for which in range(2):
                    kv[which, tiles, :, columns] = fresh[which, rows].reshape(TPP, TILE, WIDE)

        def attend(c):
            columns = pl.ds(pl.multiple_of(c * WIDE, WIDE), WIDE)
            for i in range(TPP):
                g = patch * TPP + i
                places = [tidx_ref[g, m] for m in range(TPD)]
                listed = listed_ref[g]
                keys = jnp.concatenate([kv[0, t, :, columns] for t in places], axis=0)
                values = jnp.concatenate([kv[1, t, :, columns] for t in places], axis=0)
                own = queries[i * TILE : (i + 1) * TILE, :]
                for h in range(WIDE // HEAD):
                    lanes = slice(h * HEAD, (h + 1) * HEAD)
                    score = lax.dot_general(
                        own[:, lanes],
                        keys[:, lanes],
                        (((1,), (1,)), ((), ())),
                        preferred_element_type=jnp.float32,
                    )
                    weight = jnp.exp(score * (1.0 / math.sqrt(HEAD))) * listed
                    total = jnp.sum(weight, axis=-1, keepdims=True)
                    summed = jnp.dot(
                        weight.astype(jnp.bfloat16),
                        values[:, lanes],
                        preferred_element_type=jnp.float32,
                    )
                    spot = pl.ds(pl.multiple_of(c * WIDE + h * HEAD, HEAD), HEAD)
                    attn[i * TILE : (i + 1) * TILE, spot] = (summed / total).astype(jnp.bfloat16)

        def do_heads(c, inner):
            @pl.when(beside_last)
            def _():
                first = 1 + c * per_chunk
                until = jnp.minimum(first + per_chunk, n_seq - 1)
                lax.fori_loop(first, until, forward_last, 0)

            ahead = jnp.minimum(c, CHUNKS - 1)
            project(ahead)
            attend(jnp.maximum(c - 1, 0))
            keep(ahead)
            return inner

        lax.fori_loop(0, CHUNKS + 1, do_heads, 0)

        pl.when(beside_last)(finish_last)

        def do_out(c, inner):
            columns = pl.ds(pl.multiple_of(c * WIDE, WIDE), WIDE)
            mixed = jnp.dot(attn[...], weights[c, 3], preferred_element_type=jnp.float32)
            entering = xbuf[patch, 1, :, columns].astype(jnp.float32)
            out_ref[patch, :, columns] = (entering + mixed).astype(jnp.bfloat16)
            return inner

        lax.fori_loop(0, CHUNKS, do_out, 0)

        @pl.when(has_next)
        def _():
            pl.when(has_left)(lambda: x_copy(out_ref, patch, -1, seg + 1).start())
            pl.when(has_right)(lambda: x_copy(out_ref, patch, 1, seg + 1).start())
            x_copy(out_ref, patch, 0, seg + 1).start()

        return carry

    def latent_left(patch, carry):
        pl.when(has_left)(lambda: x_copy(latent_ref, patch, -1, seg).wait_send())
        pl.when(has_right)(lambda: x_copy(latent_ref, patch, 1, seg).wait_send())
        return carry

    @pl.when(seg == 0)
    def _():
        lax.fori_loop(0, PATCHES, latent_left, 0)

    lax.fori_loop(0, PATCHES, do_patch, 0)

    def drain_ring(step, carry):
        for part, way in parts:
            ring_copy(step, way, part).wait_send()
        for way in range(2):
            last_copy(step, way).wait_send()
        return carry

    lax.fori_loop(0, n_seq - 1, drain_ring, 0)
    stale_copy().wait_send()

    def drain_x(patch, carry):
        x_copy(out_ref, patch, 0, seg + 1).wait_send()
        pl.when(has_left)(lambda: x_copy(out_ref, patch, -1, seg + 1).wait_send())
        pl.when(has_right)(lambda: x_copy(out_ref, patch, 1, seg + 1).wait_send())
        return carry

    @pl.when(has_next)
    def _():
        lax.fori_loop(0, PATCHES, drain_x, 0)


def per_device(
    n_seg,
    n_seq,
    latent,
    stale_kv,
    query_weight,
    key_weight,
    value_weight,
    out_weight,
    query_gain,
    key_gain,
    tile_mask,
):
    tok_dev = latent.shape[0]
    patch_rows = tok_dev // PATCHES
    tiles_dev = tile_mask.shape[0]
    seq = lax.axis_index("seq")
    usable = tile_mask >= 0
    own = tiles_dev + jnp.arange(tiles_dev, dtype=jnp.int32)[:, None]
    tidx = jnp.where(usable, tile_mask - (seq - 1) * tiles_dev, own)
    listed = jnp.repeat(usable, TILE, axis=1).astype(jnp.float32)[:, None, :]
    vmem = pl.BlockSpec(memory_space=pltpu.VMEM)
    smem = pl.BlockSpec(memory_space=pltpu.SMEM)
    anywhere = pl.BlockSpec(memory_space=pl.ANY)
    steps = n_seq - 1
    dma = pltpu.SemaphoreType.DMA
    result = pl.pallas_call(
        functools.partial(kernel, n_seg, n_seq),
        out_shape=jax.ShapeDtypeStruct((PATCHES, patch_rows, D), jnp.bfloat16),
        in_specs=[smem, vmem, vmem, vmem, vmem] + [anywhere] * 5,
        out_specs=vmem,
        scratch_shapes=[
            pltpu.VMEM((CHUNKS, MATS, D, WIDE), jnp.bfloat16),
            pltpu.VMEM((2, 3 * tiles_dev, TILE, D), jnp.bfloat16),
            pltpu.VMEM((PATCHES, 3, patch_rows, D), jnp.bfloat16),
            pltpu.VMEM((patch_rows, D), jnp.bfloat16),
            pltpu.VMEM((patch_rows, WIDE), jnp.bfloat16),
            pltpu.VMEM((patch_rows, WIDE), jnp.bfloat16),
            pltpu.VMEM((2, 3 * patch_rows, WIDE), jnp.bfloat16),
            dma((MATS * CHUNKS,)),
            dma,
            dma((2, steps, LANE_CHUNKS)),
            dma((2, steps, LANE_CHUNKS)),
            dma((2, steps)),
            dma((2, steps)),
            pltpu.SemaphoreType.REGULAR,
            dma((2,)),
            dma((2,)),
            dma((PATCHES, 3)),
            dma((PATCHES, 3)),
        ],
        compiler_params=pltpu.CompilerParams(
            collective_id=0, has_side_effects=True, vmem_limit_bytes=56 * 1024 * 1024
        ),
    )(
        tidx,
        listed,
        query_gain,
        key_gain,
        latent.reshape(PATCHES, patch_rows, D),
        stale_kv[0].reshape(2, tiles_dev, TILE, D),
        query_weight[0],
        key_weight[0],
        value_weight[0],
        out_weight[0],
    )
    return result.reshape(1, tok_dev, D)


def solution(mesh):
    return jax.shard_map(
        functools.partial(per_device, mesh.shape["segment"], mesh.shape["seq"]),
        mesh=mesh,
        in_specs=(
            P("seq", None),
            P("segment", None, "seq", None),
            P("segment", "seq", None),
            P("segment", "seq", None),
            P("segment", "seq", None),
            P("segment", "seq", None),
            P("segment", None),
            P("segment", None),
            P("seq", None),
        ),
        out_specs=P("segment", "seq", None),
        check_vma=False,
    )
```
